128 devices in a mesh: view: 4 (over z_lo, core), brick: 32 (over z_hi, x, y).
Axes of the slice: x: 4, y: 4, z: 4 (z_hi: 2, z_lo: 2; z = z_hi * 2 + z_lo), core: 2. Of those that a mesh axis runs over, the one named last changes fastest.
Arguments:
- start_estimate: float32 [1024, 256, 128], P('brick'), may hold values from 0.5 to 2
- observed: bfloat16 [4, 1024, 256, 128], P('view', 'brick'), may hold values from 0.25 to 4
- psf_taps: float32 [4, 3, 3, 15], P('view'), may hold values from 0.01 to 0.15
- offsets: int32 [4], P('view'), may hold values from 0 to 31
- coverage: int32 [4, 32], P(None, 'brick'), may hold values from 0 to 1, as said below
Outputs:
- estimate: float32 [1024, 256, 128], P('brick')
The draws below stay inside these ranges and needn't reach their ends.
Inputs may be any that keep to these rules, and one draw needn't show every extreme that they name: `coverage`: each brick is covered by at least one view.
All inputs are finite; a program needn't handle non-finite values.
Results may differ from the reference program's by a relative error of at most 0.0003.
Values may be sent and summed in bfloat16 or wider, within the bound.
No kernel may reach another device: no remote copies, remote signals or barrier semaphores. Data moves between devices by JAX's collectives and lax.ppermute only.
A program may use at most 128 MiB of HBM per device.

```python
import math
import jax
import jax.numpy as jnp
from jax import lax

BX = 32
NY = 256
NZ = 128
TAPS = 15
RANK = 3
ITERS = 2
VIEWS = 4
BRICKS = 32
NX = 1024


def draw_coverage(key, part):
    key = jax.random.fold_in(key, 5)
    first_key, second_key = jax.random.split(key)
    random_bits = jax.random.randint(first_key, (VIEWS, BRICKS), 0, 2)
    anchors = jax.random.randint(second_key, (1, BRICKS), 0, VIEWS)
    view_rows = lax.broadcasted_iota(jnp.int32, (VIEWS, BRICKS), 0)
    return jnp.maximum(random_bits, (view_rows == anchors).astype(jnp.int32))


def touch_ends(values, rng, least, high):
    shape = values.shape
    index_at = [jax.random.randint(jax.random.fold_in(rng, axis), (), 0, shape[axis]) for axis in range(len(shape))]
    values = values.at[tuple(index_at)].set(least)
    longest = shape.index(max(shape))
    index_at[longest] = (index_at[longest] + 1) % shape[longest]
    return values.at[tuple(index_at)].set(high)


def level_of(key, shape, cuts, smallest, high):
    def one(dim, shards_of):
        steps = jax.random.uniform(jax.random.fold_in(jax.random.fold_in(key, 6), dim), (shards_of,), jnp.float32, smallest / len(cuts), high / len(cuts))
        return jnp.repeat(jnp.exp(steps), shape[dim] // shards_of).reshape((-1,) + (1,) * (len(shape) - dim - 1))

    factor_of = one(*cuts[0])
    for cut in cuts[1:]:
        factor_of = factor_of * one(*cut)
    return factor_of


def setup_inputs(seed: int = 0) -> dict:
    key_of = jax.random.split(jax.random.key(seed), 6)
    return {
        "start_estimate": jnp.clip(jnp.exp(math.log(2.0) - 1.3862944 * jax.random.uniform(key_of[0], (NX, NY, NZ), jnp.float32) ** level_of(key_of[0], (NX, NY, NZ), ((0, 32),), -0.2, 0.2)), 0.5, 2.0),
        "observed": jnp.clip(jnp.exp(math.log(4.0) - 2.7725887 * jax.random.uniform(key_of[1], (VIEWS, NX, NY, NZ), jnp.float32) ** level_of(key_of[1], (VIEWS, NX, NY, NZ), ((0, 4), (1, 32)), -0.2, 0.2)), 0.25, 4.0).astype(jnp.bfloat16),
        "psf_taps": jnp.clip(jnp.exp(math.log(0.15) - 2.7080503 * jax.random.uniform(key_of[2], (VIEWS, 3, RANK, TAPS), jnp.float32) ** level_of(key_of[2], (VIEWS, 3, RANK, TAPS), ((0, 4),), -0.2, 0.2)), 0.01, 0.15),
        "offsets": touch_ends(jax.random.randint(key_of[3], (VIEWS,), 0, BX), jax.random.fold_in(key_of[3], 1), 0, BX - 1).astype(jnp.int32),
        "coverage": draw_coverage(jax.random.fold_in(key_of[5], 71), 0),
    }


def along_axis(volume, kernel, axis, flipped):
    tap_count = kernel.shape[0]
    half_width = tap_count // 2
    extent = volume.shape[axis]
    padding = [(0, 0), (0, 0), (0, 0)]
    padding[axis] = (half_width, half_width)
    padded = jnp.pad(volume, padding)
    summed = jnp.zeros_like(volume)
    for tap_index in range(tap_count):
        root = tap_count - 1 - tap_index if flipped else tap_index
        summed = summed + kernel[tap_index] * lax.slice_in_dim(padded, root, root + extent, axis=axis)
    return summed


def separable(volume, kernels, flipped):
    summed = jnp.zeros_like(volume)
    for member in range(kernels.shape[1]):
        along_x = along_axis(volume, kernels[0, member], 0, flipped)
        along_y = along_axis(along_x, kernels[1, member], 1, flipped)
        summed = summed + along_axis(along_y, kernels[2, member], 2, flipped)
    return summed


def reference(start_estimate, observed, psf_taps, offsets, coverage):
    weights = jnp.repeat(coverage.astype(jnp.float32), BX, axis=1)
    counts = jnp.sum(weights, axis=0)[:, None, None]
    padded_views = jnp.concatenate([observed, observed[:, :BX]], axis=1)
    estimate = start_estimate
    for iteration in range(ITERS):
        def one_view(view_index):
            merged_view = lax.dynamic_slice_in_dim(padded_views[view_index], offsets[view_index].astype(jnp.int32), NX, 0)
            blurred = separable(estimate, psf_taps[view_index], False)
            quotient = merged_view.astype(jnp.float32) / blurred
            adjoint_term = separable(quotient, psf_taps[view_index], True)
            return weights[view_index][:, None, None] * adjoint_term

        terms = lax.map(one_view, jnp.arange(observed.shape[0], dtype=jnp.int32))
        summed = jnp.sum(terms, axis=0)
        estimate = estimate * summed / counts
    return estimate
```

```python
import jax
import jax.numpy as jnp
from jax import lax
from jax.experimental import pallas as pl
from jax.experimental.pallas import tpu as pltpu
from jax.sharding import PartitionSpec as P

BX, NY, NZ = 32, 256, 128
VIEWS, RANK, TAPS = 4, 3, 15
QY = NY // VIEWS
HX = TAPS // 2
HY = 8
EX, EY = BX + 2 * HX, QY + 2 * HY
PAIRS = VIEWS * RANK
YB = 16
YW = 32
FX = 2
FW = FX + TAPS - 1
AX = 4
AW = AX + TAPS - 1
KINDS = (0, 1, 2, 6, 7)
VMEM_LIMIT = 56 * 1024 * 1024


def split(value):
    high = value.astype(jnp.bfloat16)
    return high, (value - high.astype(jnp.float32)).astype(jnp.bfloat16)


def bands(kernels, rows, cols, shift):
    taps_at = lax.broadcasted_iota(jnp.int32, (rows, cols, TAPS), 2)
    rows_at = lax.broadcasted_iota(jnp.int32, (rows, cols, TAPS), 0)
    cols_at = lax.broadcasted_iota(jnp.int32, (rows, cols, TAPS), 1)
    picked = cols_at - rows_at - shift == taps_at
    return jnp.sum(jnp.where(picked, kernels[..., None, None, :], 0.0), axis=-1)


def plane_matrices(taps):
    along_x = taps[:, 0].reshape(PAIRS, TAPS)
    along_y = taps[:, 1].reshape(PAIRS, TAPS)
    y_band = bands(along_y, YB, YW, 1)
    x_forward = bands(along_x, FX, FW, 0)
    forward = x_forward[:, :, None, :, None] * y_band[:, None, :, None, :]
    forward = forward.astype(jnp.bfloat16).reshape(PAIRS * FX * YB, FW * YW)
    x_adjoint = jnp.transpose(bands(along_x, AX, AW, 0), (2, 0, 1))
    y_adjoint = jnp.transpose(y_band, (2, 0, 1))
    adjoint = x_adjoint[:, None, :, :, None] * y_adjoint[None, :, :, None, :]
    adjoint = adjoint.astype(jnp.bfloat16).reshape(AW * YW, PAIRS * AX * YB)
    return forward, adjoint


def weighted_planes(adjoint, weights):
    tops = jnp.arange(BX // AX)[jnp.array(KINDS)][:, None] * AX + jnp.arange(AW)[None, :]
    side = jnp.where(tops < HX, 0, jnp.where(tops < HX + BX, 1, 2))
    scale = jnp.where(side[..., None] == 1, weights[1], jnp.where(side[..., None] == 0, weights[0], weights[2]))
    scale = scale.astype(jnp.bfloat16)[:, :, None, :, None]
    scaled = scale * adjoint.reshape(1, AW, YW, VIEWS, RANK * AX * YB)
    return scaled.reshape(len(KINDS), AW * YW, PAIRS * AX * YB)


def line_matrices(taps):
    along_z = taps[:, 2]
    transposed = bands(along_z, NZ, NZ, -(TAPS // 2))
    high, low = split(jnp.swapaxes(transposed, 2, 3))
    forward = jnp.concatenate([high, low], axis=3).reshape(VIEWS, RANK * NZ, 2 * NZ)
    high, low = split(transposed)
    stacked = jnp.concatenate([high, low], axis=2)
    adjoint = jnp.transpose(stacked, (0, 2, 1, 3)).reshape(VIEWS, 2 * NZ, RANK * NZ)
    return forward, adjoint


def forward_plane(ext_ref, plane_ref, mid_ref):
    @pl.loop(0, BX // (2 * FX))
    def _(step):
        x0 = step * (2 * FX)
        for y0 in range(0, QY, YB):
            parts = [
                ext_ref[pl.ds(x0 + part * FX, FW), y0 : y0 + YW, :].reshape(FW * YW, NZ)
                for part in range(2)
            ]
            made = jnp.dot(
                plane_ref[...],
                jnp.concatenate(parts, axis=1),
                preferred_element_type=jnp.float32,
            ).astype(jnp.bfloat16)
            for view in range(VIEWS):
                for term in range(RANK):
                    for part in range(2):
                        for dx in range(FX):
                            row = ((view * RANK + term) * FX + dx) * YB
                            mid_ref[
                                view, x0 + part * FX + dx, y0 : y0 + YB, term * NZ : (term + 1) * NZ
                            ] = made[row : row + YB, part * NZ : (part + 1) * NZ]


def forward_line(mid_ref, line_ref, view, x0, rows):
    a = mid_ref[view, pl.ds(x0, rows)].reshape(rows * QY, RANK * NZ)
    made = jnp.dot(a, line_ref[view], preferred_element_type=jnp.float32)
    return made[:, :NZ] + made[:, NZ:]


def merged_row(offset, here_ref, next_ref, view, x):
    at = offset + x
    here = here_ref[view, jnp.minimum(at, BX - 1)].astype(jnp.float32)
    after = next_ref[view, jnp.maximum(at - BX, 0)].astype(jnp.float32)
    return jnp.where(at < BX, here, after)


def adjoint_line(quotient, line_ref, back_ref, view, x0, rows):
    doubled = jnp.concatenate([quotient, quotient], axis=1)
    made = jnp.dot(doubled, line_ref[view], preferred_element_type=jnp.float32).astype(jnp.bfloat16)
    for term in range(RANK):
        back_ref[view * RANK + term, pl.ds(x0, rows)] = made[:, term * NZ : (term + 1) * NZ].reshape(
            rows, QY, NZ
        )


def adjoint_plane(back_ref, plane_ref, out_ref):
    out_ref[...] = jnp.zeros_like(out_ref)

    @pl.loop(0, BX // AX)
    def _(step):
        x0 = step * AX
        kind = jnp.minimum(step, 2) + jnp.maximum(step - 5, 0)
        for y0 in range(0, QY // 2, YB):
            starts = (y0, y0 + QY // 2)
            parts = [
                back_ref[:, pl.ds(x0, AX), at : at + YB, :].reshape(PAIRS * AX * YB, NZ)
                for at in starts
            ]
            made = jnp.dot(
                plane_ref[kind],
                jnp.concatenate(parts, axis=1),
                preferred_element_type=jnp.float32,
            )
            for part, at in enumerate(starts):
                out_ref[pl.ds(x0, AW), at : at + YW, :] += made[
                    :, part * NZ : (part + 1) * NZ
                ].reshape(AW, YW, NZ)


ROWS = 4


def blur_kernel(ext_ref, plane_ref, line_ref, out_ref, mid_ref):
    forward_plane(ext_ref, plane_ref, mid_ref)
    for view in range(VIEWS):

        @pl.loop(0, BX // ROWS)
        def _(step):
            x0 = step * ROWS
            blurred = forward_line(mid_ref, line_ref, view, x0, ROWS)
            out_ref[view, pl.ds(x0, ROWS)] = blurred.reshape(ROWS, QY, NZ)


def quotient_rows(offset, here_ref, next_ref, blurred, view, x0):
    merged = [merged_row(offset, here_ref, next_ref, view, x0 + row) for row in range(ROWS)]
    return (jnp.concatenate(merged, axis=0) / blurred).astype(jnp.bfloat16)


def back_kernel(
    offsets_ref, blurred_ref, here_ref, next_ref, line_ref, plane_ref, out_ref, back_ref
):
    for view in range(VIEWS):
        offset = offsets_ref[view]

        @pl.loop(0, BX // ROWS)
        def _(step):
            x0 = step * ROWS
            blurred = blurred_ref[view, pl.ds(x0, ROWS)].reshape(ROWS * QY, NZ)
            quotient = quotient_rows(offset, here_ref, next_ref, blurred, view, x0)
            adjoint_line(quotient, line_ref, back_ref, view, x0, ROWS)

    adjoint_plane(back_ref, plane_ref, out_ref)


def both_kernel(
    offsets_ref,
    ext_ref,
    here_ref,
    next_ref,
    fplane_ref,
    fline_ref,
    aline_ref,
    aplane_ref,
    out_ref,
    mid_ref,
    back_ref,
):
    forward_plane(ext_ref, fplane_ref, mid_ref)
    for view in range(VIEWS):
        offset = offsets_ref[view]

        @pl.loop(0, BX // ROWS)
        def _(step):
            x0 = step * ROWS
            blurred = forward_line(mid_ref, fline_ref, view, x0, ROWS)
            quotient = quotient_rows(offset, here_ref, next_ref, blurred, view, x0)
            adjoint_line(quotient, aline_ref, back_ref, view, x0, ROWS)

    adjoint_plane(back_ref, aplane_ref, out_ref)


VMEM = pl.BlockSpec(memory_space=pltpu.VMEM)
SMEM = pl.BlockSpec(memory_space=pltpu.SMEM)
MID = pltpu.VMEM((VIEWS, BX, QY, RANK * NZ), jnp.bfloat16)
BACK = pltpu.VMEM((PAIRS, BX, QY, NZ), jnp.bfloat16)
FLOPS = 2 * VIEWS * BX * QY * NZ * RANK * 3 * TAPS * 16


def call(kernel, out_shape, in_specs, scratch, flops, args):
    bytes_all = sum(a.size * a.dtype.itemsize for a in args)
    return pl.pallas_call(
        kernel,
        out_shape=jax.ShapeDtypeStruct(out_shape, jnp.float32),
        in_specs=in_specs,
        out_specs=VMEM,
        scratch_shapes=scratch,
        compiler_params=pltpu.CompilerParams(vmem_limit_bytes=VMEM_LIMIT),
        cost_estimate=pl.CostEstimate(flops=flops, bytes_accessed=bytes_all, transcendentals=0),
    )(*args)


def to_xor(value, by):
    return lax.ppermute(value, "view", [(i, i ^ by) for i in range(VIEWS)])


def to_next(value, axis):
    return lax.ppermute(value, axis, [(i, i + 1) for i in range(lax.axis_size(axis) - 1)])


def to_previous(value, axis):
    return lax.ppermute(value, axis, [(i + 1, i) for i in range(lax.axis_size(axis) - 1)])


def widen_x(rows):
    before = to_next(rows[BX - HX :], "brick")
    after = to_previous(rows[:HX], "brick")
    return jnp.concatenate([before, rows, after], axis=0)


def widen_y(rows):
    before = to_next(rows[:, QY - HY :], "view")
    after = to_previous(rows[:, :HY], "view")
    return jnp.concatenate([before, rows, after], axis=1)


def fold_x(wide):
    from_next = to_previous(wide[:HX], "brick")
    from_previous = to_next(wide[EX - HX :], "brick")
    own = wide[HX : HX + BX]
    return jnp.concatenate(
        [own[:HX] + from_previous, own[HX : BX - HX], own[BX - HX :] + from_next], axis=0
    )


def fold_y(wide):
    from_next = to_previous(wide[:, :HY], "view")
    from_previous = to_next(wide[:, EY - HY :], "view")
    own = wide[:, HY : HY + QY]
    return jnp.concatenate(
        [own[:, :HY] + from_previous, own[:, HY : QY - HY], own[:, QY - HY :] + from_next], axis=1
    )


def shards(start_estimate, observed, psf_taps, offsets, coverage):
    me = lax.axis_index("view")
    small = jnp.concatenate([psf_taps.reshape(-1), offsets.astype(jnp.float32)])[None]
    smalls = jnp.concatenate([small] + [to_xor(small, by) for by in range(1, VIEWS)], axis=0)

    tile = observed[0]
    here, after = [], []
    bricks = lax.axis_size("brick")
    for by in range(VIEWS):
        piece = lax.dynamic_slice_in_dim(tile, QY * (me ^ by), QY, 1)
        piece = to_xor(piece, by) if by else piece
        here.append(piece)
        after.append(lax.ppermute(piece, "brick", [((i + 1) % bricks, i) for i in range(bricks)]))

    padded = jnp.pad(start_estimate, ((0, 0), (HY, HY), (0, 0)))
    wide = lax.dynamic_slice_in_dim(padded, QY * me, EY, 1)
    estimate = wide[:, HY : HY + QY]
    ext = widen_x(wide.astype(jnp.bfloat16))

    taps = smalls[:, : 3 * RANK * TAPS].reshape(VIEWS, 3, RANK, TAPS)
    shifts = smalls[:, 3 * RANK * TAPS].astype(jnp.int32)
    covered = coverage[:, 0].astype(jnp.float32)
    count = jnp.sum(covered)
    covers = jnp.stack([to_next(covered, "brick"), covered, to_previous(covered, "brick")])
    weights = jnp.concatenate(
        [lax.dynamic_slice_in_dim(covers, me ^ by, 1, 1) for by in range(VIEWS)], axis=1
    )
    fplane, aplane = plane_matrices(taps)
    aplane = weighted_planes(aplane, weights)
    fline, aline = line_matrices(taps)

    blurred = call(
        blur_kernel, (VIEWS, BX, QY, NZ), [VMEM] * 3, [MID], FLOPS, (ext, fplane, fline)
    )
    here, after = jnp.stack(here), jnp.stack(after)
    terms = call(
        back_kernel,
        (EX, EY, NZ),
        [SMEM] + [VMEM] * 5,
        [BACK],
        FLOPS,
        (shifts, blurred, here, after, aline, aplane),
    )
    estimate = estimate * fold_y(fold_x(terms)) / count

    ext = widen_x(widen_y(estimate.astype(jnp.bfloat16)))
    terms = call(
        both_kernel,
        (EX, EY, NZ),
        [SMEM] + [VMEM] * 7,
        [MID, BACK],
        2 * FLOPS,
        (shifts, ext, here, after, fplane, fline, aline, aplane),
    )
    estimate = estimate * fold_y(fold_x(terms)) / count

    across = to_xor(estimate, 2)
    quarters = [estimate, to_xor(estimate, 1), across, to_xor(across, 1)]
    result = jnp.zeros(start_estimate.shape, jnp.float32)
    for by in range(VIEWS):
        result = lax.dynamic_update_slice_in_dim(result, quarters[by], QY * (me ^ by), 1)
    return result


def solution(mesh):
    in_specs = (
        P("brick", None, None),
        P("view", "brick", None, None),
        P("view", None, None, None),
        P("view"),
        P(None, "brick"),
    )
    out_specs = P("brick", None, None)
    return jax.shard_map(shards, mesh=mesh, in_specs=in_specs, out_specs=out_specs, check_vma=False)
```

```python
import functools

import jax
import jax.numpy as jnp
from jax import lax
from jax.experimental import pallas as pl
from jax.experimental.pallas import tpu as pltpu
from jax.sharding import PartitionSpec as P

BX, NY, NZ = 32, 256, 128
VIEWS, RANK, TAPS = 4, 3, 15
QY = NY // VIEWS
HX = TAPS // 2
HY = 8
EX, EY = BX + 2 * HX, QY + 2 * HY
PAIRS = VIEWS * RANK
YB = 16
YW = 32
FX = 2
FW = FX + TAPS - 1
AX = 4
AW = AX + TAPS - 1
KINDS = (0, 1, 2, 6, 7)
ROWS = 8
HALF = VIEWS // 2
VMEM_LIMIT = 56 * 1024 * 1024
KX, KY, KZ, OFFSET = (d * RANK * TAPS for d in range(4))


def iota(shape, dim):
    return lax.broadcasted_iota(jnp.int32, shape, dim)


def split(value):
    high = value.astype(jnp.bfloat16)
    return high, (value - high.astype(jnp.float32)).astype(jnp.bfloat16)


def prepare_kernel(small_ref, weights_ref, fplane_ref, aplane_ref, fline_ref, aline_ref):
    def tap(base, pair, t):
        return small_ref[pair // RANK, base + (pair % RANK) * TAPS + t]

    lane = iota((YB, 128), 1)
    t_y = (lane & (YW - 1)) - iota((YB, 128), 0) - 1
    group = lane >> 5
    for pair in range(PAIRS):
        y = jnp.zeros((YB, 128), jnp.float32)
        for t in range(TAPS):
            y = jnp.where(t_y == t, tap(KY, pair, t), y)
        for dx in range(FX):
            for column in range(FW * YW // 128):
                x = jnp.zeros((YB, 128), jnp.float32)
                for j in range(4):
                    t = 4 * column + j - dx
                    if 0 <= t < TAPS:
                        x = jnp.where(group == j, tap(KX, pair, t), x)
                row = (pair * FX + dx) * YB
                fplane_ref[row : row + YB, column * 128 : column * 128 + 128] = (x * y).astype(jnp.bfloat16)

    lane = iota((YW, 128), 1)
    t_y = iota((YW, 128), 0) - (lane & (YB - 1)) - 1
    group = lane >> 4
    for column in range(PAIRS // 2):
        pairs = (2 * column, 2 * column + 1)
        first = group < AX
        y = jnp.zeros((YW, 128), jnp.float32)
        for t in range(TAPS):
            y = jnp.where(t_y == t, jnp.where(first, tap(KY, pairs[0], t), tap(KY, pairs[1], t)), y)
        sided = [
            y * jnp.where(first, weights_ref[side, pairs[0] // RANK], weights_ref[side, pairs[1] // RANK])
            for side in range(3)
        ]
        for xw in range(AW):
            x = jnp.zeros((YW, 128), jnp.float32)
            for half in range(2):
                for dx in range(AX):
                    if 0 <= xw - dx < TAPS:
                        x = jnp.where(group == half * AX + dx, tap(KX, pairs[half], xw - dx), x)
            made = {}
            for kind, step in enumerate(KINDS):
                row = step * AX + xw
                side = 0 if row < HX else 1 if row < HX + BX else 2
                if side not in made:
                    made[side] = (x * sided[side]).astype(jnp.bfloat16)
                aplane_ref[kind, xw * YW : xw * YW + YW, column * 128 : column * 128 + 128] = made[side]

    t_z = iota((NZ, NZ), 0) - iota((NZ, NZ), 1) + TAPS // 2

    @pl.loop(0, VIEWS)
    def _(view):
        for term in range(RANK):
            forward = jnp.zeros((NZ, NZ), jnp.float32)
            adjoint = jnp.zeros((NZ, NZ), jnp.float32)
            for t in range(TAPS):
                k = small_ref[view, KZ + term * TAPS + t]
                forward = jnp.where(t_z == t, k, forward)
                adjoint = jnp.where(t_z == TAPS - 1 - t, k, adjoint)
            at = term * NZ
            high, low = split(forward)
            fline_ref[view, at : at + NZ, :NZ] = high
            fline_ref[view, at : at + NZ, NZ:] = low
            high, low = split(adjoint)
            aline_ref[view, :NZ, at : at + NZ] = high
            aline_ref[view, NZ:, at : at + NZ] = low


def forward_plane(ext_ref, plane_ref, mid_ref):
    @pl.loop(0, BX // (2 * FX))
    def _(step):
        x0 = step * (2 * FX)
        for y0 in range(0, QY, YB):
            parts = [
                ext_ref[pl.ds(x0 + part * FX, FW), y0 : y0 + YW, :].reshape(FW * YW, NZ)
                for part in range(2)
            ]
            made = jnp.dot(
                plane_ref[...],
                jnp.concatenate(parts, axis=1),
                preferred_element_type=jnp.float32,
            ).astype(jnp.bfloat16)
            for view in range(VIEWS):
                for term in range(RANK):
                    for part in range(2):
                        for dx in range(FX):
                            row = ((view * RANK + term) * FX + dx) * YB
                            mid_ref[
                                view, x0 + part * FX + dx, y0 : y0 + YB, term * NZ : (term + 1) * NZ
                            ] = made[row : row + YB, part * NZ : (part + 1) * NZ]


def forward_line(mid_ref, line_ref, view, x0):
    a = mid_ref[view, pl.ds(x0, ROWS)].reshape(ROWS * QY, RANK * NZ)
    made = jnp.dot(a, line_ref[view], preferred_element_type=jnp.float32)
    return made[:, :NZ] + made[:, NZ:]


def quotient_rows(tiles_ref, slot, start, blurred):
    merged = tiles_ref[slot, pl.ds(start, ROWS)].reshape(ROWS * QY, NZ)
    return (merged.astype(jnp.float32) / blurred).astype(jnp.bfloat16)


def adjoint_line(quotient, line_ref, back_ref, view, slot, x0):
    doubled = jnp.concatenate([quotient, quotient], axis=1)
    made = jnp.dot(doubled, line_ref[view], preferred_element_type=jnp.float32).astype(jnp.bfloat16)
    for term in range(RANK):
        back_ref[slot * RANK + term, pl.ds(x0, ROWS)] = made[:, term * NZ : (term + 1) * NZ].reshape(
            ROWS, QY, NZ
        )


def adjoint_plane(back_ref, plane_ref, out_ref, first_pair, pairs):
    columns = slice(first_pair * AX * YB, (first_pair + pairs) * AX * YB)

    @pl.loop(0, BX // AX)
    def _(step):
        x0 = step * AX
        kind = jnp.minimum(step, 2) + jnp.maximum(step - 5, 0)
        for y0 in range(0, QY // 2, YB):
            starts = (y0, y0 + QY // 2)
            parts = [
                back_ref[:pairs, pl.ds(x0, AX), at : at + YB, :].reshape(pairs * AX * YB, NZ)
                for at in starts
            ]
            made = jnp.dot(
                plane_ref[kind, :, columns],
                jnp.concatenate(parts, axis=1),
                preferred_element_type=jnp.float32,
            )
            for part, at in enumerate(starts):
                out_ref[pl.ds(x0, AW), at : at + YW, :] += made[
                    :, part * NZ : (part + 1) * NZ
                ].reshape(AW, YW, NZ)


def edges(out_ref, up_ref, down_ref):
    rows = up_ref.shape[0]
    up_ref[...] = out_ref[:rows]
    down_ref[...] = out_ref[EX - rows :]


def blur_kernel(ext_ref, plane_ref, line_hbm, first_ref, last_ref, mid_ref, line_ref, sem):
    copy = pltpu.make_async_copy(line_hbm, line_ref, sem.at[0])
    copy.start()
    forward_plane(ext_ref, plane_ref, mid_ref)
    copy.wait()
    for view in range(VIEWS):
        out_ref = (first_ref, last_ref)[view // HALF]

        @pl.loop(0, BX // ROWS)
        def _(step):
            x0 = step * ROWS
            blurred = forward_line(mid_ref, line_ref, view, x0)
            out_ref[view % HALF, pl.ds(x0, ROWS)] = blurred.reshape(ROWS, QY, NZ)


def back_kernel(first_view, begun, edge_rows, *refs):
    refs = list(refs)
    offsets_ref, blurred_hbm = refs[:2]
    tiles_hbm = refs[2 : 2 + 2 * HALF]
    line_ref, plane_hbm = refs[2 + 2 * HALF : 4 + 2 * HALF]
    rest = refs[4 + 2 * HALF :]
    before_ref = rest.pop(0) if begun else None
    out_refs = [rest.pop(0) for _ in range(3 if begun else 1)]
    blurred_ref, tiles_ref, plane_ref, back_ref, sems = rest
    out_ref = out_refs[0]
    copies = [
        [pltpu.make_async_copy(blurred_hbm.at[slot], blurred_ref.at[slot], sems.at[slot])]
        + [
            pltpu.make_async_copy(
                tiles_hbm[2 * slot + part],
                tiles_ref.at[slot, pl.ds(part * BX, BX)],
                sems.at[HALF + 2 * slot + part],
            )
            for part in range(2)
        ]
        for slot in range(HALF)
    ]
    plane_copy = pltpu.make_async_copy(plane_hbm, plane_ref, sems.at[3 * HALF])
    for copy in copies[0] + copies[1] + [plane_copy]:
        copy.start()
    out_ref[...] = before_ref[...] if begun else jnp.zeros_like(out_ref)
    for slot in range(HALF):
        view = first_view + slot
        offset = offsets_ref[view]
        for copy in copies[slot]:
            copy.wait()

        @pl.loop(0, BX // ROWS)
        def _(step):
            x0 = step * ROWS
            blurred = blurred_ref[slot, pl.ds(x0, ROWS)].reshape(ROWS * QY, NZ)
            quotient = quotient_rows(tiles_ref, slot, offset + x0, blurred)
            adjoint_line(quotient, line_ref, back_ref, view, slot, x0)

    plane_copy.wait()
    adjoint_plane(back_ref, plane_ref, out_ref, first_view * RANK, HALF * RANK)
    if begun:
        edges(*out_refs)


def both_kernel(offsets_ref, ext_ref, fplane_ref, fline_hbm, aline_hbm, aplane_hbm, *refs):
    tiles_hbm = refs[: 2 * VIEWS]
    out_ref, up_ref, down_ref, mid_ref, back_ref, fline_ref, aline_ref, aplane_ref, tiles_ref, sems = refs[
        2 * VIEWS :
    ]
    line_copies = [
        pltpu.make_async_copy(fline_hbm, fline_ref, sems.at[0]),
        pltpu.make_async_copy(aline_hbm, aline_ref, sems.at[1]),
    ]
    plane_copy = pltpu.make_async_copy(aplane_hbm, aplane_ref, sems.at[2])
    tile_copies = [
        pltpu.make_async_copy(
            tiles_hbm[2 * view + part], tiles_ref.at[view, pl.ds(part * BX, BX)], sems.at[3 + 2 * view + part]
        )
        for view in range(VIEWS)
        for part in range(2)
    ]
    for copy in line_copies + tile_copies + [plane_copy]:
        copy.start()
    out_ref[...] = jnp.zeros_like(out_ref)
    forward_plane(ext_ref, fplane_ref, mid_ref)
    for copy in line_copies + tile_copies:
        copy.wait()
    for view in range(VIEWS):
        offset = offsets_ref[view]

        @pl.loop(0, BX // ROWS)
        def _(step):
            x0 = step * ROWS
            blurred = forward_line(mid_ref, fline_ref, view, x0)
            quotient = quotient_rows(tiles_ref, view, offset + x0, blurred)
            adjoint_line(quotient, aline_ref, back_ref, view, view, x0)

    plane_copy.wait()
    adjoint_plane(back_ref, aplane_ref, out_ref, 0, PAIRS)
    edges(out_ref, up_ref, down_ref)


VMEM = pl.BlockSpec(memory_space=pltpu.VMEM)
SMEM = pl.BlockSpec(memory_space=pltpu.SMEM)
ANY = pl.BlockSpec(memory_space=pl.ANY)
F32, BF16 = jnp.float32, jnp.bfloat16
FPLANE = ((PAIRS * FX * YB, FW * YW), BF16)
APLANE = ((len(KINDS), AW * YW, PAIRS * AX * YB), BF16)
FLINE = ((VIEWS, RANK * NZ, 2 * NZ), BF16)
ALINE = ((VIEWS, 2 * NZ, RANK * NZ), BF16)
MID = ((VIEWS, BX, QY, RANK * NZ), BF16)
SUMS = ((EX, EY, NZ), F32)
FLOPS = 2 * VIEWS * BX * QY * NZ * RANK * 3 * TAPS * 16


def call(kernel, outs, in_specs, scratch, flops, args):
    bytes_all = sum(a.size * a.dtype.itemsize for a in args)
    return pl.pallas_call(
        kernel,
        out_shape=[jax.ShapeDtypeStruct(*out) for out in outs],
        in_specs=in_specs,
        out_specs=[VMEM] * len(outs),
        scratch_shapes=[
            pltpu.SemaphoreType.DMA((s,)) if isinstance(s, int) else pltpu.VMEM(*s) for s in scratch
        ],
        compiler_params=pltpu.CompilerParams(vmem_limit_bytes=VMEM_LIMIT),
        cost_estimate=pl.CostEstimate(flops=flops, bytes_accessed=bytes_all, transcendentals=0),
    )(*args)


def to_xor(value, by):
    return lax.ppermute(value, "view", [(i, i ^ by) for i in range(VIEWS)])


def exchange(axis, to_previous, to_next):
    up = [(i, i + 1) for i in range(lax.axis_size(axis) - 1)]
    from_previous = lax.ppermute(to_next, axis, up)
    from_next = lax.ppermute(to_previous, axis, [(j, i) for i, j in up])
    return lax.optimization_barrier((from_previous, from_next))


def fold(value, from_previous, from_next, dim, skip):
    width, size = from_next.shape[dim], value.shape[dim]
    pads = [[(0, 0)] * 3 for _ in range(2)]
    pads[0][dim] = (skip, size - width - skip)
    pads[1][dim] = (size - width - skip, skip)
    return value + jnp.pad(from_previous, pads[0]) + jnp.pad(from_next, pads[1])


def shards(start_estimate, observed, psf_taps, offsets, coverage):
    me = lax.axis_index("view")
    bricks = lax.axis_size("brick")

    pieces = [lax.dynamic_slice_in_dim(observed[0], QY * (me ^ by), QY, 1) for by in range(VIEWS)]
    pieces, start_estimate, psf_taps, coverage = lax.optimization_barrier(
        (pieces, start_estimate, psf_taps, coverage)
    )
    tiles = []
    for by, piece in enumerate(pieces):
        piece = to_xor(piece, by) if by else piece
        tiles.append((piece, lax.ppermute(piece, "brick", [((i + 1) % bricks, i) for i in range(bricks)])))

    small = jnp.concatenate([psf_taps.reshape(-1), offsets.astype(F32)])[None]
    smalls = jnp.concatenate([small] + [to_xor(small, by) for by in range(1, VIEWS)], axis=0)
    shifts = smalls[:, OFFSET].astype(jnp.int32)
    covered = coverage[:, 0].astype(F32)
    before, after = exchange("brick", covered, covered)
    covers = jnp.stack([before, covered, after])
    weights = jnp.concatenate(
        [lax.dynamic_slice_in_dim(covers, me ^ by, 1, 1) for by in range(VIEWS)], axis=1
    )
    counts = jnp.maximum(jnp.sum(covers, axis=1), 1.0)
    row_counts = jnp.concatenate(
        [jnp.full((HX,), counts[0]), jnp.full((BX,), counts[1]), jnp.full((HX,), counts[2])]
    )[:, None, None]
    fplane, aplane, fline, aline = call(
        prepare_kernel, [FPLANE, APLANE, FLINE, ALINE], [SMEM, SMEM], [], 10**9, (smalls, weights)
    )

    padded = jnp.pad(start_estimate, ((0, 0), (HY, HY), (0, 0)))
    estimate = lax.dynamic_slice_in_dim(padded, QY * me, EY, 1)
    edge = estimate.astype(BF16)
    before, after = exchange("brick", edge[:HX], edge[BX - HX :])
    estimate = jnp.concatenate([before.astype(F32), estimate, after.astype(F32)], axis=0)

    half = ((HALF, BX, QY, NZ), F32)
    blurred = call(
        blur_kernel,
        [half, half],
        [VMEM, VMEM, ANY],
        [MID, FLINE, 1],
        FLOPS,
        (estimate.astype(BF16), fplane, fline),
    )
    tile_scratch = lambda views: ((views, 2 * BX, QY, NZ), BF16)
    back_scratch = lambda views: ((views * RANK, BX, QY, NZ), BF16)
    terms = ()
    for part in range(2):
        first_view = part * HALF
        outs = [SUMS, ((2 * HX, EY, NZ), F32), ((2 * HX, EY, NZ), F32)] if part else [SUMS]
        own_tiles = [tile for pair in tiles[first_view : first_view + HALF] for tile in pair]
        terms = call(
            functools.partial(back_kernel, first_view, part == 1, 2 * HX),
            outs,
            [SMEM] + [ANY] * (1 + 2 * HALF) + [VMEM, ANY] + [VMEM] * part,
            [half, tile_scratch(HALF), APLANE, back_scratch(HALF), 3 * HALF + 1],
            FLOPS // 2,
            (shifts, blurred[part], *own_tiles, aline, aplane, *terms),
        )
    summed, to_previous, to_next = terms
    summed = fold(summed, *exchange("brick", to_previous, to_next), 0, 0)
    summed = fold(summed, *exchange("view", summed[:, : 2 * HY], summed[:, QY:]), 1, 0)
    estimate = estimate * summed / row_counts

    summed, to_previous, to_next = call(
        both_kernel,
        [SUMS, ((HX, EY, NZ), F32), ((HX, EY, NZ), F32)],
        [SMEM, VMEM, VMEM] + [ANY] * (3 + 2 * VIEWS),
        [MID, back_scratch(VIEWS), FLINE, ALINE, APLANE, tile_scratch(VIEWS), 3 + 2 * VIEWS],
        2 * FLOPS,
        (shifts, estimate.astype(BF16), fplane, fline, aline, aplane, *[tile for pair in tiles for tile in pair]),
    )
    summed = fold(summed[HX : HX + BX], *exchange("brick", to_previous, to_next), 0, 0)
    summed = fold(
        summed[:, HY : HY + QY], *exchange("view", summed[:, :HY], summed[:, EY - HY :]), 1, 0
    )
    estimate = estimate[HX : HX + BX, HY : HY + QY] * summed / counts[1]

    across = to_xor(estimate, 2)
    quarters = [estimate, to_xor(estimate, 1), across, to_xor(across, 1)]
    result = jnp.zeros(start_estimate.shape, F32)
    for by in range(VIEWS):
        result = lax.dynamic_update_slice_in_dim(result, quarters[by], QY * (me ^ by), 1)
    return result


def solution(mesh):
    in_specs = (
        P("brick", None, None),
        P("view", "brick", None, None),
        P("view", None, None, None),
        P("view"),
        P(None, "brick"),
    )
    out_specs = P("brick", None, None)
    return jax.shard_map(shards, mesh=mesh, in_specs=in_specs, out_specs=out_specs, check_vma=False)
```

```python
import functools

import jax
import jax.numpy as jnp
from jax import lax
from jax.experimental import pallas as pl
from jax.experimental.pallas import tpu as pltpu
from jax.sharding import PartitionSpec as P

BX, NY, NZ = 32, 256, 128
VIEWS, RANK, TAPS = 4, 3, 15
QY = NY // VIEWS
HX = TAPS // 2
HY = 8
EX, EY = BX + 2 * HX, QY + 2 * HY
PAIRS = VIEWS * RANK
YB = 16
YW = 32
FX = 2
FW = FX + TAPS - 1
AX = 4
AW = AX + TAPS - 1
KINDS = (0, 1, 2, 6, 7)
ROWS = 8
HALF = VIEWS // 2
VMEM_LIMIT = 56 * 1024 * 1024
KX, KY, KZ, OFFSET = (d * RANK * TAPS for d in range(4))


def iota(shape, dim):
    return lax.broadcasted_iota(jnp.int32, shape, dim)


def split(value):
    high = value.astype(jnp.bfloat16)
    return high, (value - high.astype(jnp.float32)).astype(jnp.bfloat16)


def prepare_kernel(first_ref, small_ref, covers_ref, fplane_ref, aplane_ref, fline_ref, aline_ref):
    me = first_ref[0]

    def tap(base, pair, t):
        return small_ref[pair // RANK, base + (pair % RANK) * TAPS + t]

    def weight(side, pair):
        return covers_ref[side, me ^ (pair // RANK)]

    lane = iota((YB, 128), 1)
    t_y = (lane & (YW - 1)) - iota((YB, 128), 0) - 1
    group = lane >> 5
    for pair in range(PAIRS):
        y = jnp.zeros((YB, 128), jnp.float32)
        for t in range(TAPS):
            y = jnp.where(t_y == t, tap(KY, pair, t), y)
        for dx in range(FX):
            for column in range(FW * YW // 128):
                x = jnp.zeros((YB, 128), jnp.float32)
                for j in range(4):
                    t = 4 * column + j - dx
                    if 0 <= t < TAPS:
                        x = jnp.where(group == j, tap(KX, pair, t), x)
                row = (pair * FX + dx) * YB
                fplane_ref[row : row + YB, column * 128 : column * 128 + 128] = (x * y).astype(jnp.bfloat16)

    lane = iota((YW, 128), 1)
    t_y = iota((YW, 128), 0) - (lane & (YB - 1)) - 1
    group = lane >> 4
    for column in range(PAIRS // 2):
        pairs = (2 * column, 2 * column + 1)
        first = group < AX
        y = jnp.zeros((YW, 128), jnp.float32)
        for t in range(TAPS):
            y = jnp.where(t_y == t, jnp.where(first, tap(KY, pairs[0], t), tap(KY, pairs[1], t)), y)
        sided = [
            y * jnp.where(first, weight(side, pairs[0]), weight(side, pairs[1])) for side in range(3)
        ]
        for xw in range(AW):
            x = jnp.zeros((YW, 128), jnp.float32)
            for half in range(2):
                for dx in range(AX):
                    if 0 <= xw - dx < TAPS:
                        x = jnp.where(group == half * AX + dx, tap(KX, pairs[half], xw - dx), x)
            made = {}
            for kind, step in enumerate(KINDS):
                row = step * AX + xw
                side = 0 if row < HX else 1 if row < HX + BX else 2
                if side not in made:
                    made[side] = (x * sided[side]).astype(jnp.bfloat16)
                aplane_ref[kind, xw * YW : xw * YW + YW, column * 128 : column * 128 + 128] = made[side]

    t_z = iota((NZ, NZ), 0) - iota((NZ, NZ), 1) + TAPS // 2

    @pl.loop(0, VIEWS)
    def _(view):
        for term in range(RANK):
            forward = jnp.zeros((NZ, NZ), jnp.float32)
            adjoint = jnp.zeros((NZ, NZ), jnp.float32)
            for t in range(TAPS):
                k = small_ref[view, KZ + term * TAPS + t]
                forward = jnp.where(t_z == t, k, forward)
                adjoint = jnp.where(t_z == TAPS - 1 - t, k, adjoint)
            at = term * NZ
            high, low = split(forward)
            fline_ref[view, at : at + NZ, :NZ] = high
            fline_ref[view, at : at + NZ, NZ:] = low
            high, low = split(adjoint)
            aline_ref[view, :NZ, at : at + NZ] = high
            aline_ref[view, NZ:, at : at + NZ] = low


def forward_plane(ext_ref, plane_ref, mid_ref):
    @pl.loop(0, BX // (2 * FX))
    def _(step):
        x0 = step * (2 * FX)
        for y0 in range(0, QY, YB):
            parts = [
                ext_ref[pl.ds(x0 + part * FX, FW), y0 : y0 + YW, :].reshape(FW * YW, NZ)
                for part in range(2)
            ]
            made = jnp.dot(
                plane_ref[...],
                jnp.concatenate(parts, axis=1),
                preferred_element_type=jnp.float32,
            ).astype(jnp.bfloat16)
            for view in range(VIEWS):
                for term in range(RANK):
                    for part in range(2):
                        for dx in range(FX):
                            row = ((view * RANK + term) * FX + dx) * YB
                            mid_ref[
                                view, x0 + part * FX + dx, y0 : y0 + YB, term * NZ : (term + 1) * NZ
                            ] = made[row : row + YB, part * NZ : (part + 1) * NZ]


def forward_line(mid_ref, line_ref, view, x0):
    a = mid_ref[view, pl.ds(x0, ROWS)].reshape(ROWS * QY, RANK * NZ)
    made = jnp.dot(a, line_ref[view], preferred_element_type=jnp.float32)
    return made[:, :NZ] + made[:, NZ:]


def quotient_rows(tiles_ref, slot, start, blurred):
    merged = tiles_ref[slot, pl.ds(start, ROWS)].reshape(ROWS * QY, NZ)
    return (merged.astype(jnp.float32) / blurred).astype(jnp.bfloat16)


def adjoint_line(quotient, line_ref, back_ref, view, slot, x0):
    doubled = jnp.concatenate([quotient, quotient], axis=1)
    made = jnp.dot(doubled, line_ref[view], preferred_element_type=jnp.float32).astype(jnp.bfloat16)
    for term in range(RANK):
        back_ref[slot * RANK + term, pl.ds(x0, ROWS)] = made[:, term * NZ : (term + 1) * NZ].reshape(
            ROWS, QY, NZ
        )


def adjoint_plane(back_ref, plane_ref, out_ref, first_pair, pairs):
    columns = slice(first_pair * AX * YB, (first_pair + pairs) * AX * YB)

    @pl.loop(0, BX // AX)
    def _(step):
        x0 = step * AX
        kind = jnp.minimum(step, 2) + jnp.maximum(step - 5, 0)
        for y0 in range(0, QY // 2, YB):
            starts = (y0, y0 + QY // 2)
            parts = [
                back_ref[:pairs, pl.ds(x0, AX), at : at + YB, :].reshape(pairs * AX * YB, NZ)
                for at in starts
            ]
            made = jnp.dot(
                plane_ref[kind, :, columns],
                jnp.concatenate(parts, axis=1),
                preferred_element_type=jnp.float32,
            )
            for part, at in enumerate(starts):
                out_ref[pl.ds(x0, AW), at : at + YW, :] += made[
                    :, part * NZ : (part + 1) * NZ
                ].reshape(AW, YW, NZ)


def edges(out_ref, up_ref, down_ref):
    rows = up_ref.shape[0]
    up_ref[...] = out_ref[:rows]
    down_ref[...] = out_ref[EX - rows :]


def tile_copy(tile_hbm, rows_ref, part, sem):
    return pltpu.make_async_copy(tile_hbm.at[pl.ds(0, BX)], rows_ref.at[pl.ds(part * BX, BX)], sem)


def blur_kernel(ext_ref, plane_ref, line_hbm, first_ref, last_ref, mid_ref, line_ref, sem):
    copy = pltpu.make_async_copy(line_hbm, line_ref, sem.at[0])
    copy.start()
    forward_plane(ext_ref, plane_ref, mid_ref)
    copy.wait()
    for view in range(VIEWS):
        out_ref = (first_ref, last_ref)[view // HALF]

        @pl.loop(0, BX // ROWS)
        def _(step):
            x0 = step * ROWS
            blurred = forward_line(mid_ref, line_ref, view, x0)
            out_ref[view % HALF, pl.ds(x0, ROWS)] = blurred.reshape(ROWS, QY, NZ)


def back_kernel(first_view, begun, edge_rows, *refs):
    refs = list(refs)
    offsets_ref, blurred_hbm = refs[:2]
    tiles_hbm = refs[2 : 2 + 2 * HALF]
    line_ref, plane_hbm = refs[2 + 2 * HALF : 4 + 2 * HALF]
    rest = refs[4 + 2 * HALF :]
    before_ref = rest.pop(0) if begun else None
    out_refs = [rest.pop(0) for _ in range(3 if begun else 1)]
    blurred_ref, tiles_ref, plane_ref, back_ref, sems = rest
    out_ref = out_refs[0]
    copies = [
        [pltpu.make_async_copy(blurred_hbm.at[slot], blurred_ref.at[slot], sems.at[slot])]
        + [
            tile_copy(tiles_hbm[2 * slot + part], tiles_ref.at[slot], part, sems.at[HALF + 2 * slot + part])
            for part in range(2)
        ]
        for slot in range(HALF)
    ]
    plane_copy = pltpu.make_async_copy(plane_hbm, plane_ref, sems.at[3 * HALF])
    for copy in copies[0] + copies[1] + [plane_copy]:
        copy.start()
    out_ref[...] = before_ref[...] if begun else jnp.zeros_like(out_ref)
    for slot in range(HALF):
        view = first_view + slot
        offset = offsets_ref[view]
        for copy in copies[slot]:
            copy.wait()

        @pl.loop(0, BX // ROWS)
        def _(step):
            x0 = step * ROWS
            blurred = blurred_ref[slot, pl.ds(x0, ROWS)].reshape(ROWS * QY, NZ)
            quotient = quotient_rows(tiles_ref, slot, offset + x0, blurred)
            adjoint_line(quotient, line_ref, back_ref, view, slot, x0)

    plane_copy.wait()
    adjoint_plane(back_ref, plane_ref, out_ref, first_view * RANK, HALF * RANK)
    if begun:
        edges(*out_refs)


def both_kernel(offsets_ref, ext_ref, fplane_ref, fline_hbm, aline_hbm, aplane_hbm, *refs):
    tiles_hbm = refs[: 2 * VIEWS]
    out_ref, up_ref, down_ref, mid_ref, back_ref, fline_ref, aline_ref, aplane_ref, tiles_ref, sems = refs[
        2 * VIEWS :
    ]
    line_copies = [
        pltpu.make_async_copy(fline_hbm, fline_ref, sems.at[0]),
        pltpu.make_async_copy(aline_hbm, aline_ref, sems.at[1]),
    ]
    plane_copy = pltpu.make_async_copy(aplane_hbm, aplane_ref, sems.at[2])
    tile_copies = [
        tile_copy(tiles_hbm[2 * view + part], tiles_ref.at[view], part, sems.at[3 + 2 * view + part])
        for view in range(VIEWS)
        for part in range(2)
    ]
    for copy in line_copies + tile_copies + [plane_copy]:
        copy.start()
    out_ref[...] = jnp.zeros_like(out_ref)
    forward_plane(ext_ref, fplane_ref, mid_ref)
    for copy in line_copies + tile_copies:
        copy.wait()
    for view in range(VIEWS):
        offset = offsets_ref[view]

        @pl.loop(0, BX // ROWS)
        def _(step):
            x0 = step * ROWS
            blurred = forward_line(mid_ref, fline_ref, view, x0)
            quotient = quotient_rows(tiles_ref, view, offset + x0, blurred)
            adjoint_line(quotient, aline_ref, back_ref, view, view, x0)

    plane_copy.wait()
    adjoint_plane(back_ref, aplane_ref, out_ref, 0, PAIRS)
    edges(out_ref, up_ref, down_ref)


VMEM = pl.BlockSpec(memory_space=pltpu.VMEM)
SMEM = pl.BlockSpec(memory_space=pltpu.SMEM)
ANY = pl.BlockSpec(memory_space=pl.ANY)
F32, BF16 = jnp.float32, jnp.bfloat16
FPLANE = ((PAIRS * FX * YB, FW * YW), BF16)
APLANE = ((len(KINDS), AW * YW, PAIRS * AX * YB), BF16)
FLINE = ((VIEWS, RANK * NZ, 2 * NZ), BF16)
ALINE = ((VIEWS, 2 * NZ, RANK * NZ), BF16)
MID = ((VIEWS, BX, QY, RANK * NZ), BF16)
SUMS = ((EX, EY, NZ), F32)
FLOPS = 2 * VIEWS * BX * QY * NZ * RANK * 3 * TAPS * 16


def call(kernel, outs, in_specs, scratch, flops, args):
    bytes_all = sum(a.size * a.dtype.itemsize for a in args)
    return pl.pallas_call(
        kernel,
        out_shape=[jax.ShapeDtypeStruct(*out) for out in outs],
        in_specs=in_specs,
        out_specs=[VMEM] * len(outs),
        scratch_shapes=[
            pltpu.SemaphoreType.DMA((s,)) if isinstance(s, int) else pltpu.VMEM(*s) for s in scratch
        ],
        compiler_params=pltpu.CompilerParams(vmem_limit_bytes=VMEM_LIMIT),
        cost_estimate=pl.CostEstimate(flops=flops, bytes_accessed=bytes_all, transcendentals=0),
    )(*args)


def place(quarter, brick, bricks):
    return (quarter ^ (2 if brick >= bricks // 2 else 0)) * bricks + brick


def send(value, pairs):
    bricks = lax.axis_size("brick")
    perm = [(place(*a, bricks), place(*b, bricks)) for a, b in pairs]
    return lax.ppermute(value, ("view", "brick"), perm)


def to_xor(value, by):
    return lax.ppermute(value, "view", [(i, i ^ by) for i in range(VIEWS)])


def from_next_brick(value):
    bricks = lax.axis_size("brick")
    return send(value, [((q, (b + 1) % bricks), (q, b)) for b in range(bricks) for q in range(VIEWS)])


def exchange(axis, to_previous, to_next):
    bricks = lax.axis_size("brick")
    if axis == "brick":
        up = [((q, b), (q, b + 1)) for b in range(bricks - 1) for q in range(VIEWS)]
    else:
        up = [((q, b), (q + 1, b)) for b in range(bricks) for q in range(VIEWS - 1)]
    from_previous = send(to_next, up)
    from_next = send(to_previous, [(j, i) for i, j in up])
    return lax.optimization_barrier((from_previous, from_next))


def fold(value, from_previous, from_next, dim, skip):
    width, size = from_next.shape[dim], value.shape[dim]
    pads = [[(0, 0)] * 3 for _ in range(2)]
    pads[0][dim] = (skip, size - width - skip)
    pads[1][dim] = (size - width - skip, skip)
    return value + jnp.pad(from_previous, pads[0]) + jnp.pad(from_next, pads[1])


def in_bf16(values):
    rows = []
    for _ in range(3):
        rows.append(lax.reduce_precision(values, 8, 7))
        values = values - rows[-1]
    return jnp.stack(rows).astype(BF16)


def shards(start_estimate, observed, psf_taps, offsets, coverage):
    me = lax.axis_index("view")
    bricks = lax.axis_size("brick")
    quarter = me ^ (2 * (lax.axis_index("brick") // (bricks // 2)))

    small = jnp.concatenate([psf_taps.reshape(-1), offsets.astype(F32)])
    wide = -(-small.shape[0] // NZ)
    row = in_bf16(jnp.pad(small, (0, wide * NZ - small.shape[0]))).reshape(1, 3 * wide, NZ)
    row = jnp.pad(row, ((0, 0), (0, QY - 3 * wide), (0, 0)))
    pieces = [lax.dynamic_slice_in_dim(observed[0], QY * (quarter ^ by), QY, 1) for by in range(VIEWS)]
    pieces = [jnp.concatenate([piece, row], axis=0) for piece in pieces]
    start_estimate, pieces = lax.optimization_barrier((start_estimate, pieces))
    here = [to_xor(piece, by) if by else piece for by, piece in enumerate(pieces)]
    beyond = [from_next_brick(tile) for tile in here]
    across = lax.rem(lax.axis_index("brick") + 1, bricks // 2) == 0
    here = [jnp.where(across, here[by ^ 2], here[by]) for by in range(VIEWS)]
    first = jnp.where(across, me ^ 2, me)
    tiles = list(zip(here, beyond))
    smalls = jnp.concatenate([tile[BX:] for tile in here], axis=0)[:, : 3 * wide].astype(F32).reshape(VIEWS, 3, wide * NZ)
    smalls = (smalls[:, 2] + smalls[:, 1]) + smalls[:, 0]
    shifts = smalls[:, OFFSET].astype(jnp.int32)

    padded = jnp.pad(start_estimate, ((0, 0), (HY, HY), (0, 0)))
    estimate = lax.dynamic_slice_in_dim(padded, QY * quarter, EY, 1)
    edge = estimate.astype(BF16)
    covered = jnp.broadcast_to(coverage.reshape(1, VIEWS, 1).astype(BF16), (1, VIEWS, NZ))
    covered = jnp.pad(covered, ((0, 0), (0, EY - VIEWS), (0, 0)))
    before, after = exchange(
        "brick",
        jnp.concatenate([edge[:HX], covered], axis=0),
        jnp.concatenate([edge[BX - HX :], covered], axis=0),
    )
    covers = jnp.stack([rows[HX, :VIEWS, 0] for rows in (before, jnp.pad(covered, ((HX, 0), (0, 0), (0, 0))), after)])
    covers = covers.astype(F32)
    counts = jnp.maximum(jnp.sum(covers, axis=1), 1.0)
    row_counts = jnp.repeat(counts, jnp.array([HX, BX, HX]), total_repeat_length=EX)[:, None, None]
    estimate = jnp.concatenate([before[:HX].astype(F32), estimate, after[:HX].astype(F32)], axis=0)
    fplane, aplane, fline, aline = call(
        prepare_kernel, [FPLANE, APLANE, FLINE, ALINE], [SMEM] * 3, [], 10**9, (first[None], smalls, covers)
    )

    half = ((HALF, BX, QY, NZ), F32)
    blurred = call(
        blur_kernel,
        [half, half],
        [VMEM, VMEM, ANY],
        [MID, FLINE, 1],
        FLOPS,
        (estimate.astype(BF16), fplane, fline),
    )
    tile_scratch = lambda views: ((views, 2 * BX, QY, NZ), BF16)
    back_scratch = lambda views: ((views * RANK, BX, QY, NZ), BF16)
    terms = ()
    for part in range(2):
        first_view = part * HALF
        outs = [SUMS, ((2 * HX, EY, NZ), F32), ((2 * HX, EY, NZ), F32)] if part else [SUMS]
        own_tiles = [tile for pair in tiles[first_view : first_view + HALF] for tile in pair]
        terms = call(
            functools.partial(back_kernel, first_view, part == 1, 2 * HX),
            outs,
            [SMEM] + [ANY] * (1 + 2 * HALF) + [VMEM, ANY] + [VMEM] * part,
            [half, tile_scratch(HALF), APLANE, back_scratch(HALF), 3 * HALF + 1],
            FLOPS // 2,
            (shifts, blurred[part], *own_tiles, aline, aplane, *terms),
        )
    summed, to_previous, to_next = terms
    summed = fold(summed, *exchange("brick", to_previous, to_next), 0, 0)
    summed = fold(summed, *exchange("view", summed[:, : 2 * HY], summed[:, QY:]), 1, 0)
    estimate = estimate * summed / row_counts

    summed, to_previous, to_next = call(
        both_kernel,
        [SUMS, ((HX, EY, NZ), F32), ((HX, EY, NZ), F32)],
        [SMEM, VMEM, VMEM] + [ANY] * (3 + 2 * VIEWS),
        [MID, back_scratch(VIEWS), FLINE, ALINE, APLANE, tile_scratch(VIEWS), 3 + 2 * VIEWS],
        2 * FLOPS,
        (shifts, estimate.astype(BF16), fplane, fline, aline, aplane, *[tile for pair in tiles for tile in pair]),
    )
    summed = fold(summed[HX : HX + BX], *exchange("brick", to_previous, to_next), 0, 0)
    summed = fold(
        summed[:, HY : HY + QY], *exchange("view", summed[:, :HY], summed[:, EY - HY :]), 1, 0
    )
    estimate = estimate[HX : HX + BX, HY : HY + QY] * summed / counts[1]

    across = to_xor(estimate, 2)
    quarters = [estimate, to_xor(estimate, 1), across, to_xor(across, 1)]
    result = jnp.zeros(start_estimate.shape, F32)
    for by in range(VIEWS):
        result = lax.dynamic_update_slice_in_dim(result, quarters[by], QY * (quarter ^ by), 1)
    return result


def solution(mesh):
    in_specs = (
        P("brick", None, None),
        P("view", "brick", None, None),
        P("view", None, None, None),
        P("view"),
        P(None, "brick"),
    )
    out_specs = P("brick", None, None)
    return jax.shard_map(shards, mesh=mesh, in_specs=in_specs, out_specs=out_specs, check_vma=False)
```

```python
import functools

import jax
import jax.numpy as jnp
from jax import lax
from jax.experimental import pallas as pl
from jax.experimental.pallas import tpu as pltpu
from jax.sharding import PartitionSpec as P

BX, NY, NZ = 32, 256, 128
VIEWS, RANK, TAPS = 4, 3, 15
QY = NY // VIEWS
HX = TAPS // 2
HY = 8
EX, EY = BX + 2 * HX, QY + 2 * HY
PAIRS = VIEWS * RANK
YB = 16
YW = 32
FX = 2
FW = FX + TAPS - 1
AX = 4
AW = AX + TAPS - 1
KINDS = (0, 1, 2, 6, 7)
ROWS = 8
HALF = VIEWS // 2
VMEM_LIMIT = 56 * 1024 * 1024
KX, KY, KZ, OFFSET = (d * RANK * TAPS for d in range(4))


def iota(shape, dim):
    return lax.broadcasted_iota(jnp.int32, shape, dim)


def split(value):
    high = value.astype(jnp.bfloat16)
    return high, (value - high.astype(jnp.float32)).astype(jnp.bfloat16)


def prepare_kernel(first_ref, small_ref, covers_ref, fplane_ref, aplane_ref, fline_ref, aline_ref):
    me = first_ref[0]

    def tap(base, pair, t):
        return small_ref[pair // RANK, base + (pair % RANK) * TAPS + t]

    def weight(side, pair):
        return covers_ref[side, me ^ (pair // RANK)]

    lane = iota((YB, 128), 1)
    t_y = (lane & (YW - 1)) - iota((YB, 128), 0) - 1
    group = lane >> 5
    for pair in range(PAIRS):
        y = jnp.zeros((YB, 128), jnp.float32)
        for t in range(TAPS):
            y = jnp.where(t_y == t, tap(KY, pair, t), y)
        for dx in range(FX):
            for column in range(FW * YW // 128):
                x = jnp.zeros((YB, 128), jnp.float32)
                for j in range(4):
                    t = 4 * column + j - dx
                    if 0 <= t < TAPS:
                        x = jnp.where(group == j, tap(KX, pair, t), x)
                row = (pair * FX + dx) * YB
                fplane_ref[row : row + YB, column * 128 : column * 128 + 128] = (x * y).astype(jnp.bfloat16)

    lane = iota((YW, 128), 1)
    t_y = iota((YW, 128), 0) - (lane & (YB - 1)) - 1
    group = lane >> 4
    for column in range(PAIRS // 2):
        pairs = (2 * column, 2 * column + 1)
        first = group < AX
        y = jnp.zeros((YW, 128), jnp.float32)
        for t in range(TAPS):
            y = jnp.where(t_y == t, jnp.where(first, tap(KY, pairs[0], t), tap(KY, pairs[1], t)), y)
        sided = [
            y * jnp.where(first, weight(side, pairs[0]), weight(side, pairs[1])) for side in range(3)
        ]
        for xw in range(AW):
            x = jnp.zeros((YW, 128), jnp.float32)
            for half in range(2):
                for dx in range(AX):
                    if 0 <= xw - dx < TAPS:
                        x = jnp.where(group == half * AX + dx, tap(KX, pairs[half], xw - dx), x)
            made = {}
            for kind, step in enumerate(KINDS):
                row = step * AX + xw
                side = 0 if row < HX else 1 if row < HX + BX else 2
                if side not in made:
                    made[side] = (x * sided[side]).astype(jnp.bfloat16)
                aplane_ref[kind, xw * YW : xw * YW + YW, column * 128 : column * 128 + 128] = made[side]

    t_z = iota((NZ, NZ), 0) - iota((NZ, NZ), 1) + TAPS // 2

    @pl.loop(0, VIEWS)
    def _(view):
        for term in range(RANK):
            forward = jnp.zeros((NZ, NZ), jnp.float32)
            adjoint = jnp.zeros((NZ, NZ), jnp.float32)
            for t in range(TAPS):
                k = small_ref[view, KZ + term * TAPS + t]
                forward = jnp.where(t_z == t, k, forward)
                adjoint = jnp.where(t_z == TAPS - 1 - t, k, adjoint)
            at = term * NZ
            high, low = split(forward)
            fline_ref[view, at : at + NZ, :NZ] = high
            fline_ref[view, at : at + NZ, NZ:] = low
            high, low = split(adjoint)
            aline_ref[view, :NZ, at : at + NZ] = high
            aline_ref[view, NZ:, at : at + NZ] = low


def forward_plane(ext_ref, plane_ref, mid_ref):
    @pl.loop(0, BX // (2 * FX))
    def _(step):
        x0 = step * (2 * FX)
        for y0 in range(0, QY, YB):
            parts = [
                ext_ref[pl.ds(x0 + part * FX, FW), y0 : y0 + YW, :].reshape(FW * YW, NZ)
                for part in range(2)
            ]
            made = jnp.dot(
                plane_ref[...],
                jnp.concatenate(parts, axis=1),
                preferred_element_type=jnp.float32,
            ).astype(jnp.bfloat16)
            for view in range(VIEWS):
                for term in range(RANK):
                    for part in range(2):
                        for dx in range(FX):
                            row = ((view * RANK + term) * FX + dx) * YB
                            mid_ref[
                                view, x0 + part * FX + dx, y0 : y0 + YB, term * NZ : (term + 1) * NZ
                            ] = made[row : row + YB, part * NZ : (part + 1) * NZ]


def forward_line(mid_ref, line_ref, view, x0):
    a = mid_ref[view, pl.ds(x0, ROWS)].reshape(ROWS * QY, RANK * NZ)
    made = jnp.dot(a, line_ref[view], preferred_element_type=jnp.float32)
    return made[:, :NZ] + made[:, NZ:]


def quotient_rows(tiles_ref, slot, start, blurred):
    merged = tiles_ref[slot, pl.ds(start, ROWS)].reshape(ROWS * QY, NZ)
    return (merged.astype(jnp.float32) / blurred).astype(jnp.bfloat16)


def adjoint_line(quotient, line_ref, back_ref, view, slot, x0):
    doubled = jnp.concatenate([quotient, quotient], axis=1)
    made = jnp.dot(doubled, line_ref[view], preferred_element_type=jnp.float32).astype(jnp.bfloat16)
    for term in range(RANK):
        back_ref[slot * RANK + term, pl.ds(x0, ROWS)] = made[:, term * NZ : (term + 1) * NZ].reshape(
            ROWS, QY, NZ
        )


def adjoint_plane(back_ref, plane_ref, out_ref, first_pair, pairs):
    columns = slice(first_pair * AX * YB, (first_pair + pairs) * AX * YB)

    @pl.loop(0, BX // AX)
    def _(step):
        x0 = step * AX
        kind = jnp.minimum(step, 2) + jnp.maximum(step - 5, 0)
        for y0 in range(0, QY // 2, YB):
            starts = (y0, y0 + QY // 2)
            parts = [
                back_ref[:pairs, pl.ds(x0, AX), at : at + YB, :].reshape(pairs * AX * YB, NZ)
                for at in starts
            ]
            made = jnp.dot(
                plane_ref[kind, :, columns],
                jnp.concatenate(parts, axis=1),
                preferred_element_type=jnp.float32,
            )
            for part, at in enumerate(starts):
                out_ref[pl.ds(x0, AW), at : at + YW, :] += made[
                    :, part * NZ : (part + 1) * NZ
                ].reshape(AW, YW, NZ)


def edges(out_ref, up_ref, down_ref):
    rows = up_ref.shape[0]
    up_ref[...] = out_ref[:rows]
    down_ref[...] = out_ref[EX - rows :]


def tile_copy(tile_hbm, rows_ref, part, sem):
    return pltpu.make_async_copy(tile_hbm.at[pl.ds(0, BX)], rows_ref.at[pl.ds(part * BX, BX)], sem)


def blur_kernel(ext_ref, plane_ref, line_hbm, first_ref, last_ref, mid_ref, line_ref, sem):
    copy = pltpu.make_async_copy(line_hbm, line_ref, sem.at[0])
    copy.start()
    forward_plane(ext_ref, plane_ref, mid_ref)
    copy.wait()
    for view in range(VIEWS):
        out_ref = (first_ref, last_ref)[view // HALF]

        @pl.loop(0, BX // ROWS)
        def _(step):
            x0 = step * ROWS
            blurred = forward_line(mid_ref, line_ref, view, x0)
            out_ref[view % HALF, pl.ds(x0, ROWS)] = blurred.reshape(ROWS, QY, NZ)


def back_kernel(first_view, begun, edge_rows, *refs):
    refs = list(refs)
    offsets_ref, blurred_hbm = refs[:2]
    tiles_hbm = refs[2 : 2 + 2 * HALF]
    line_ref, plane_hbm = refs[2 + 2 * HALF : 4 + 2 * HALF]
    rest = refs[4 + 2 * HALF :]
    before_ref = rest.pop(0) if begun else None
    out_refs = [rest.pop(0) for _ in range(3 if begun else 1)]
    blurred_ref, tiles_ref, plane_ref, back_ref, sems = rest
    out_ref = out_refs[0]
    copies = [
        [pltpu.make_async_copy(blurred_hbm.at[slot], blurred_ref.at[slot], sems.at[slot])]
        + [
            tile_copy(tiles_hbm[2 * slot + part], tiles_ref.at[slot], part, sems.at[HALF + 2 * slot + part])
            for part in range(2)
        ]
        for slot in range(HALF)
    ]
    plane_copy = pltpu.make_async_copy(plane_hbm, plane_ref, sems.at[3 * HALF])
    for copy in copies[0] + copies[1] + [plane_copy]:
        copy.start()
    out_ref[...] = before_ref[...] if begun else jnp.zeros_like(out_ref)
    for slot in range(HALF):
        view = first_view + slot
        offset = offsets_ref[view]
        for copy in copies[slot]:
            copy.wait()

        @pl.loop(0, BX // ROWS)
        def _(step):
            x0 = step * ROWS
            blurred = blurred_ref[slot, pl.ds(x0, ROWS)].reshape(ROWS * QY, NZ)
            quotient = quotient_rows(tiles_ref, slot, offset + x0, blurred)
            adjoint_line(quotient, line_ref, back_ref, view, slot, x0)

    plane_copy.wait()
    adjoint_plane(back_ref, plane_ref, out_ref, first_view * RANK, HALF * RANK)
    if begun:
        edges(*out_refs)


def both_kernel(offsets_ref, ext_ref, fplane_ref, fline_hbm, aline_hbm, aplane_hbm, *refs):
    tiles_hbm = refs[: 2 * VIEWS]
    out_ref, up_ref, down_ref, mid_ref, back_ref, fline_ref, aline_ref, aplane_ref, tiles_ref, sems = refs[
        2 * VIEWS :
    ]
    line_copies = [
        pltpu.make_async_copy(fline_hbm, fline_ref, sems.at[0]),
        pltpu.make_async_copy(aline_hbm, aline_ref, sems.at[1]),
    ]
    plane_copy = pltpu.make_async_copy(aplane_hbm, aplane_ref, sems.at[2])
    tile_copies = [
        tile_copy(tiles_hbm[2 * view + part], tiles_ref.at[view], part, sems.at[3 + 2 * view + part])
        for view in range(VIEWS)
        for part in range(2)
    ]
    for copy in line_copies + tile_copies + [plane_copy]:
        copy.start()
    out_ref[...] = jnp.zeros_like(out_ref)
    forward_plane(ext_ref, fplane_ref, mid_ref)
    for copy in line_copies + tile_copies:
        copy.wait()
    for view in range(VIEWS):
        offset = offsets_ref[view]

        @pl.loop(0, BX // ROWS)
        def _(step):
            x0 = step * ROWS
            blurred = forward_line(mid_ref, fline_ref, view, x0)
            quotient = quotient_rows(tiles_ref, view, offset + x0, blurred)
            adjoint_line(quotient, aline_ref, back_ref, view, view, x0)

    plane_copy.wait()
    adjoint_plane(back_ref, aplane_ref, out_ref, 0, PAIRS)
    edges(out_ref, up_ref, down_ref)


VMEM = pl.BlockSpec(memory_space=pltpu.VMEM)
SMEM = pl.BlockSpec(memory_space=pltpu.SMEM)
ANY = pl.BlockSpec(memory_space=pl.ANY)
F32, BF16 = jnp.float32, jnp.bfloat16
FPLANE = ((PAIRS * FX * YB, FW * YW), BF16)
APLANE = ((len(KINDS), AW * YW, PAIRS * AX * YB), BF16)
FLINE = ((VIEWS, RANK * NZ, 2 * NZ), BF16)
ALINE = ((VIEWS, 2 * NZ, RANK * NZ), BF16)
MID = ((VIEWS, BX, QY, RANK * NZ), BF16)
SUMS = ((EX, EY, NZ), F32)
FLOPS = 2 * VIEWS * BX * QY * NZ * RANK * 3 * TAPS * 16


def call(kernel, outs, in_specs, scratch, flops, args):
    bytes_all = 1 if flops == 1 else sum(a.size * a.dtype.itemsize for a in args)
    return pl.pallas_call(
        kernel,
        out_shape=[jax.ShapeDtypeStruct(*out) for out in outs],
        in_specs=in_specs,
        out_specs=[VMEM] * len(outs),
        scratch_shapes=[
            pltpu.SemaphoreType.DMA((s,)) if isinstance(s, int) else pltpu.VMEM(*s) for s in scratch
        ],
        compiler_params=pltpu.CompilerParams(vmem_limit_bytes=VMEM_LIMIT),
        cost_estimate=pl.CostEstimate(flops=flops, bytes_accessed=bytes_all, transcendentals=0),
    )(*args)


def place(quarter, brick, bricks):
    return (quarter ^ (2 if brick >= bricks // 2 else 0)) * bricks + brick


def send(value, pairs):
    bricks = lax.axis_size("brick")
    perm = [(place(*a, bricks), place(*b, bricks)) for a, b in pairs]
    return lax.ppermute(value, ("view", "brick"), perm)


def to_xor(value, by):
    return lax.ppermute(value, "view", [(i, i ^ by) for i in range(VIEWS)])


def from_next_brick(value):
    bricks = lax.axis_size("brick")
    return send(value, [((q, (b + 1) % bricks), (q, b)) for b in range(bricks) for q in range(VIEWS)])


def exchange(axis, to_previous, to_next):
    bricks = lax.axis_size("brick")
    if axis == "brick":
        up = [((q, b), (q, b + 1)) for b in range(bricks - 1) for q in range(VIEWS)]
    else:
        up = [((q, b), (q + 1, b)) for b in range(bricks) for q in range(VIEWS - 1)]
    from_previous = send(to_next, up)
    from_next = send(to_previous, [(j, i) for i, j in up])
    return lax.optimization_barrier((from_previous, from_next))


def fold(value, from_previous, from_next, dim, skip):
    width, size = from_next.shape[dim], value.shape[dim]
    pads = [[(0, 0)] * 3 for _ in range(2)]
    pads[0][dim] = (skip, size - width - skip)
    pads[1][dim] = (size - width - skip, skip)
    return value + jnp.pad(from_previous, pads[0]) + jnp.pad(from_next, pads[1])


def gathered(own):
    across = to_xor(own, 2)
    return [own, to_xor(own, 1), across, to_xor(across, 1)]


def assemble_kernel(groups, quarter_ref, *refs):
    parts, out_ref, sems = refs[:VIEWS], refs[-2], refs[-1]
    copies = []
    for by, part in enumerate(parts):
        at = pl.multiple_of(QY * (quarter_ref[0] ^ by), QY)
        for start, row, rows in groups:
            copies.append(
                pltpu.make_async_copy(
                    part.at[pl.ds(start, rows)],
                    out_ref.at[pl.ds(row, rows), pl.ds(at, QY)],
                    sems.at[len(copies)],
                )
            )
    for copy in copies:
        copy.start()
    for copy in copies:
        copy.wait()


def assemble(quarter, parts, groups, result):
    begun = [] if result is None else [result]
    return pl.pallas_call(
        functools.partial(assemble_kernel, groups),
        out_shape=jax.ShapeDtypeStruct((BX, NY, NZ), F32),
        in_specs=[SMEM] + [ANY] * (VIEWS + len(begun)),
        out_specs=ANY,
        scratch_shapes=[pltpu.SemaphoreType.DMA((VIEWS * len(groups),))],
        input_output_aliases={1 + VIEWS: 0} if begun else {},
        compiler_params=pltpu.CompilerParams(vmem_limit_bytes=1024 * 1024),
        cost_estimate=pl.CostEstimate(flops=1, bytes_accessed=1, transcendentals=0),
    )(quarter[None], *parts, *begun)


def shards(start_estimate, observed, psf_taps, offsets, coverage):
    me = lax.axis_index("view")
    bricks = lax.axis_size("brick")
    quarter = me ^ (2 * (lax.axis_index("brick") // (bricks // 2)))

    pieces = [lax.dynamic_slice_in_dim(observed[0], QY * (quarter ^ by), QY, 1) for by in range(VIEWS)]
    here = [to_xor(piece, by) if by else piece for by, piece in enumerate(pieces)]
    here[1], start_estimate, psf_taps, offsets, coverage = lax.optimization_barrier(
        (here[1], start_estimate, psf_taps, offsets, coverage)
    )
    across = lax.rem(lax.axis_index("brick") + 1, bricks // 2) == 0
    first = jnp.where(across, me ^ 2, me)
    beyond = [from_next_brick(tile) for tile in here[:HALF]]

    smalls = jnp.concatenate([psf_taps.reshape(-1), offsets.astype(F32)])[None]
    for by in (1, 2):
        smalls = jnp.concatenate([smalls, to_xor(smalls, by)], axis=0)
    smalls = jnp.where(across, jnp.roll(smalls, HALF, axis=0), smalls)
    shifts = smalls[:, OFFSET].astype(jnp.int32)

    padded = jnp.pad(start_estimate, ((0, 0), (HY, HY), (0, 0)))
    estimate = lax.dynamic_slice_in_dim(padded, QY * quarter, EY, 1)
    edge = estimate.astype(BF16)
    covered = jnp.broadcast_to(coverage.reshape(1, VIEWS, 1).astype(BF16), (1, VIEWS, NZ))
    covered = jnp.pad(covered, ((0, 0), (0, EY - VIEWS), (0, 0)))
    before, after = exchange(
        "brick",
        jnp.concatenate([edge[:HX], covered], axis=0),
        jnp.concatenate([edge[BX - HX :], covered], axis=0),
    )
    covers = jnp.stack([rows[HX, :VIEWS, 0] for rows in (before, jnp.pad(covered, ((HX, 0), (0, 0), (0, 0))), after)])
    covers = covers.astype(F32)
    counts = jnp.maximum(jnp.sum(covers, axis=1), 1.0)
    row_counts = jnp.repeat(counts, jnp.array([HX, BX, HX]), total_repeat_length=EX)[:, None, None]
    estimate = jnp.concatenate([before[:HX].astype(F32), estimate, after[:HX].astype(F32)], axis=0)
    fplane, aplane, fline, aline = call(
        prepare_kernel, [FPLANE, APLANE, FLINE, ALINE], [SMEM] * 3, [], 1, (first[None], smalls, covers)
    )

    half = ((HALF, BX, QY, NZ), F32)
    blurred = call(
        blur_kernel,
        [half, half],
        [VMEM, VMEM, ANY],
        [MID, FLINE, 1],
        1,
        (estimate.astype(BF16), fplane, fline),
    )
    here[HALF:], beyond, blurred = lax.optimization_barrier((here[HALF:], beyond, blurred))
    beyond = beyond + [from_next_brick(tile) for tile in here[HALF:]]
    here = [jnp.where(across, here[by ^ 2], here[by]) for by in range(VIEWS)]
    tiles = list(zip(here, beyond))
    tile_scratch = lambda views: ((views, 2 * BX, QY, NZ), BF16)
    back_scratch = lambda views: ((views * RANK, BX, QY, NZ), BF16)
    terms = ()
    for part in range(2):
        first_view = part * HALF
        outs = [SUMS, ((2 * HX, EY, NZ), F32), ((2 * HX, EY, NZ), F32)] if part else [SUMS]
        own_tiles = [tile for pair in tiles[first_view : first_view + HALF] for tile in pair]
        terms = call(
            functools.partial(back_kernel, first_view, part == 1, 2 * HX),
            outs,
            [SMEM] + [ANY] * (1 + 2 * HALF) + [VMEM, ANY] + [VMEM] * part,
            [half, tile_scratch(HALF), APLANE, back_scratch(HALF), 3 * HALF + 1],
            FLOPS // 2,
            (shifts, blurred[part], *own_tiles, aline, aplane, *terms),
        )
    summed, to_previous, to_next = terms
    summed = fold(summed, *exchange("brick", to_previous, to_next), 0, 0)
    summed = fold(summed, *exchange("view", summed[:, : 2 * HY], summed[:, QY:]), 1, 0)
    estimate = estimate * summed / row_counts

    summed, to_previous, to_next = call(
        both_kernel,
        [SUMS, ((HX, EY, NZ), F32), ((HX, EY, NZ), F32)],
        [SMEM, VMEM, VMEM] + [ANY] * (3 + 2 * VIEWS),
        [MID, back_scratch(VIEWS), FLINE, ALINE, APLANE, tile_scratch(VIEWS), 3 + 2 * VIEWS],
        2 * FLOPS,
        (shifts, estimate.astype(BF16), fplane, fline, aline, aplane, *[tile for pair in tiles for tile in pair]),
    )
    own = summed[HX : HX + BX]
    inner = own[HX : BX - HX]
    from_quarters = exchange("view", inner[:, :HY], inner[:, EY - HY :])
    from_bricks = exchange("brick", to_previous, to_next)
    estimate = estimate[HX : HX + BX, HY : HY + QY] / counts[1]
    inner = estimate[HX : BX - HX] * fold(inner[:, HY : HY + QY], *from_quarters, 1, 0)
    outer = jnp.concatenate([own[:HX] + from_bricks[0], own[BX - HX :] + from_bricks[1]], axis=0)
    from_quarters = exchange("view", outer[:, :HY], outer[:, EY - HY :])
    outer = fold(outer[:, HY : HY + QY], *from_quarters, 1, 0)
    outer = jnp.concatenate([estimate[:HX], estimate[BX - HX :]], axis=0) * outer

    result = assemble(quarter, gathered(inner), ((0, HX, BX - 2 * HX),), None)
    return assemble(quarter, gathered(outer), ((0, 0, HX), (HX, BX - HX, HX)), result)


def solution(mesh):
    in_specs = (
        P("brick", None, None),
        P("view", "brick", None, None),
        P("view", None, None, None),
        P("view"),
        P(None, "brick"),
    )
    out_specs = P("brick", None, None)
    return jax.shard_map(shards, mesh=mesh, in_specs=in_specs, out_specs=out_specs, check_vma=False)
```

```python
import functools

import jax
import jax.numpy as jnp
from jax import lax
from jax.experimental import pallas as pl
from jax.experimental.pallas import tpu as pltpu
from jax.sharding import PartitionSpec as P

BX, NY, NZ = 32, 256, 128
VIEWS, RANK, TAPS = 4, 3, 15
QY = NY // VIEWS
HX = TAPS // 2
HY = 8
EX, EY = BX + 2 * HX, QY + 2 * HY
PAIRS = VIEWS * RANK
YB = 16
YW = 32
FX = 2
FW = FX + TAPS - 1
AX = 4
AW = AX + TAPS - 1
KINDS = (0, 1, 2, 6, 7)
ROWS = 8
HALF = VIEWS // 2
VMEM_LIMIT = 56 * 1024 * 1024
KX, KY, KZ, OFFSET = (d * RANK * TAPS for d in range(4))


def iota(shape, dim):
    return lax.broadcasted_iota(jnp.int32, shape, dim)


def split(value):
    high = value.astype(jnp.bfloat16)
    return high, (value - high.astype(jnp.float32)).astype(jnp.bfloat16)


def prepare_kernel(first_ref, small_ref, covers_ref, fplane_ref, aplane_ref, fline_ref, aline_ref):
    me = first_ref[0]

    def tap(base, pair, t):
        return small_ref[pair // RANK, base + (pair % RANK) * TAPS + t]

    def weight(side, pair):
        return covers_ref[side, me ^ (pair // RANK)]

    lane = iota((YB, 128), 1)
    t_y = (lane & (YW - 1)) - iota((YB, 128), 0) - 1
    group = lane >> 5
    for pair in range(PAIRS):
        y = jnp.zeros((YB, 128), jnp.float32)
        for t in range(TAPS):
            y = jnp.where(t_y == t, tap(KY, pair, t), y)
        for dx in range(FX):
            for column in range(FW * YW // 128):
                x = jnp.zeros((YB, 128), jnp.float32)
                for j in range(4):
                    t = 4 * column + j - dx
                    if 0 <= t < TAPS:
                        x = jnp.where(group == j, tap(KX, pair, t), x)
                row = (pair * FX + dx) * YB
                fplane_ref[row : row + YB, column * 128 : column * 128 + 128] = (x * y).astype(jnp.bfloat16)

    lane = iota((YW, 128), 1)
    t_y = iota((YW, 128), 0) - (lane & (YB - 1)) - 1
    group = lane >> 4
    for column in range(PAIRS // 2):
        pairs = (2 * column, 2 * column + 1)
        first = group < AX
        y = jnp.zeros((YW, 128), jnp.float32)
        for t in range(TAPS):
            y = jnp.where(t_y == t, jnp.where(first, tap(KY, pairs[0], t), tap(KY, pairs[1], t)), y)
        sided = [
            y * jnp.where(first, weight(side, pairs[0]), weight(side, pairs[1])) for side in range(3)
        ]
        for xw in range(AW):
            x = jnp.zeros((YW, 128), jnp.float32)
            for half in range(2):
                for dx in range(AX):
                    if 0 <= xw - dx < TAPS:
                        x = jnp.where(group == half * AX + dx, tap(KX, pairs[half], xw - dx), x)
            made = {}
            for kind, step in enumerate(KINDS):
                row = step * AX + xw
                side = 0 if row < HX else 1 if row < HX + BX else 2
                if side not in made:
                    made[side] = (x * sided[side]).astype(jnp.bfloat16)
                aplane_ref[kind, xw * YW : xw * YW + YW, column * 128 : column * 128 + 128] = made[side]

    t_z = iota((NZ, NZ), 0) - iota((NZ, NZ), 1) + TAPS // 2

    @pl.loop(0, VIEWS)
    def _(view):
        for term in range(RANK):
            forward = jnp.zeros((NZ, NZ), jnp.float32)
            adjoint = jnp.zeros((NZ, NZ), jnp.float32)
            for t in range(TAPS):
                k = small_ref[view, KZ + term * TAPS + t]
                forward = jnp.where(t_z == t, k, forward)
                adjoint = jnp.where(t_z == TAPS - 1 - t, k, adjoint)
            at = term * NZ
            high, low = split(forward)
            fline_ref[view, at : at + NZ, :NZ] = high
            fline_ref[view, at : at + NZ, NZ:] = low
            high, low = split(adjoint)
            aline_ref[view, :NZ, at : at + NZ] = high
            aline_ref[view, NZ:, at : at + NZ] = low


def forward_plane(ext_ref, plane_ref, mid_ref):
    @pl.loop(0, BX // (2 * FX), unroll=2)
    def _(step):
        x0 = step * (2 * FX)
        for y0 in range(0, QY, YB):
            parts = [
                ext_ref[pl.ds(x0 + part * FX, FW), y0 : y0 + YW, :].reshape(FW * YW, NZ)
                for part in range(2)
            ]
            made = jnp.dot(
                plane_ref[...],
                jnp.concatenate(parts, axis=1),
                preferred_element_type=jnp.float32,
            ).astype(jnp.bfloat16)
            for view in range(VIEWS):
                for term in range(RANK):
                    for part in range(2):
                        for dx in range(FX):
                            row = ((view * RANK + term) * FX + dx) * YB
                            mid_ref[
                                view, x0 + part * FX + dx, y0 : y0 + YB, term * NZ : (term + 1) * NZ
                            ] = made[row : row + YB, part * NZ : (part + 1) * NZ]


def forward_line(mid_ref, line_ref, view, x0):
    a = mid_ref[view, pl.ds(x0, ROWS)].reshape(ROWS * QY, RANK * NZ)
    made = jnp.dot(a, line_ref[view], preferred_element_type=jnp.float32)
    return made[:, :NZ] + made[:, NZ:]


def quotient_rows(tiles_ref, slot, start, blurred):
    merged = tiles_ref[slot, pl.ds(start, ROWS)].reshape(ROWS * QY, NZ)
    return (merged.astype(jnp.float32) / blurred).astype(jnp.bfloat16)


def adjoint_line(quotient, line_ref, back_ref, view, slot, x0):
    doubled = jnp.concatenate([quotient, quotient], axis=1)
    made = jnp.dot(doubled, line_ref[view], preferred_element_type=jnp.float32).astype(jnp.bfloat16)
    for term in range(RANK):
        back_ref[slot * RANK + term, pl.ds(x0, ROWS)] = made[:, term * NZ : (term + 1) * NZ].reshape(
            ROWS, QY, NZ
        )


def adjoint_plane(back_ref, plane_ref, out_ref, first_pair, pairs):
    columns = slice(first_pair * AX * YB, (first_pair + pairs) * AX * YB)

    for step in range(BX // AX):
        x0 = step * AX
        kind = min(step, 2) + max(step - 5, 0)
        for y0 in range(0, QY // 2, YB):
            starts = (y0, y0 + QY // 2)
            parts = [
                back_ref[:pairs, x0 : x0 + AX, at : at + YB, :].reshape(pairs * AX * YB, NZ)
                for at in starts
            ]
            made = jnp.dot(
                plane_ref[kind, :, columns],
                jnp.concatenate(parts, axis=1),
                preferred_element_type=jnp.float32,
            )
            for part, at in enumerate(starts):
                out_ref[x0 : x0 + AW, at : at + YW, :] += made[
                    :, part * NZ : (part + 1) * NZ
                ].reshape(AW, YW, NZ)


def edges(out_ref, up_ref, down_ref):
    rows = up_ref.shape[0]
    up_ref[...] = out_ref[:rows]
    down_ref[...] = out_ref[EX - rows :]


def tile_copy(tile_hbm, rows_ref, part, sem):
    return pltpu.make_async_copy(tile_hbm.at[pl.ds(0, BX)], rows_ref.at[pl.ds(part * BX, BX)], sem)


def blur_kernel(ext_ref, plane_ref, line_hbm, first_ref, last_ref, mid_ref, line_ref, sem):
    copy = pltpu.make_async_copy(line_hbm, line_ref, sem.at[0])
    copy.start()
    forward_plane(ext_ref, plane_ref, mid_ref)
    copy.wait()
    for view in range(VIEWS):
        out_ref = (first_ref, last_ref)[view // HALF]

        @pl.loop(0, BX // ROWS)
        def _(step):
            x0 = step * ROWS
            blurred = forward_line(mid_ref, line_ref, view, x0)
            out_ref[view % HALF, pl.ds(x0, ROWS)] = blurred.reshape(ROWS, QY, NZ)


def back_kernel(first_view, begun, edge_rows, *refs):
    refs = list(refs)
    offsets_ref, blurred_hbm = refs[:2]
    tiles_hbm = refs[2 : 2 + 2 * HALF]
    line_ref, plane_hbm = refs[2 + 2 * HALF : 4 + 2 * HALF]
    rest = refs[4 + 2 * HALF :]
    before_ref = rest.pop(0) if begun else None
    out_refs = [rest.pop(0) for _ in range(3 if begun else 1)]
    blurred_ref, tiles_ref, plane_ref, back_ref, sems = rest
    out_ref = out_refs[0]
    copies = [
        [pltpu.make_async_copy(blurred_hbm.at[slot], blurred_ref.at[slot], sems.at[slot])]
        + [
            tile_copy(tiles_hbm[2 * slot + part], tiles_ref.at[slot], part, sems.at[HALF + 2 * slot + part])
            for part in range(2)
        ]
        for slot in range(HALF)
    ]
    plane_copy = pltpu.make_async_copy(plane_hbm, plane_ref, sems.at[3 * HALF])
    for copy in copies[0] + copies[1] + [plane_copy]:
        copy.start()
    out_ref[...] = before_ref[...] if begun else jnp.zeros_like(out_ref)
    for slot in range(HALF):
        view = first_view + slot
        offset = offsets_ref[view]
        for copy in copies[slot]:
            copy.wait()

        @pl.loop(0, BX // ROWS)
        def _(step):
            x0 = step * ROWS
            blurred = blurred_ref[slot, pl.ds(x0, ROWS)].reshape(ROWS * QY, NZ)
            quotient = quotient_rows(tiles_ref, slot, offset + x0, blurred)
            adjoint_line(quotient, line_ref, back_ref, view, slot, x0)

    plane_copy.wait()
    adjoint_plane(back_ref, plane_ref, out_ref, first_view * RANK, HALF * RANK)
    if begun:
        edges(*out_refs)


def both_kernel(offsets_ref, ext_ref, fplane_ref, fline_hbm, aline_hbm, aplane_hbm, *refs):
    tiles_hbm = refs[: 2 * VIEWS]
    out_ref, up_ref, down_ref, mid_ref, back_ref, fline_ref, aline_ref, aplane_ref, tiles_ref, sems = refs[
        2 * VIEWS :
    ]
    line_copies = [
        pltpu.make_async_copy(fline_hbm, fline_ref, sems.at[0]),
        pltpu.make_async_copy(aline_hbm, aline_ref, sems.at[1]),
    ]
    plane_copy = pltpu.make_async_copy(aplane_hbm, aplane_ref, sems.at[2])
    tile_copies = [
        tile_copy(tiles_hbm[2 * view + part], tiles_ref.at[view], part, sems.at[3 + 2 * view + part])
        for view in range(VIEWS)
        for part in range(2)
    ]
    for copy in line_copies + tile_copies + [plane_copy]:
        copy.start()
    out_ref[...] = jnp.zeros_like(out_ref)
    forward_plane(ext_ref, fplane_ref, mid_ref)
    for copy in line_copies + tile_copies:
        copy.wait()
    for view in range(VIEWS):
        offset = offsets_ref[view]

        @pl.loop(0, BX // ROWS)
        def _(step):
            x0 = step * ROWS
            blurred = forward_line(mid_ref, fline_ref, view, x0)
            quotient = quotient_rows(tiles_ref, view, offset + x0, blurred)
            adjoint_line(quotient, aline_ref, back_ref, view, view, x0)

    plane_copy.wait()
    adjoint_plane(back_ref, aplane_ref, out_ref, 0, PAIRS)
    edges(out_ref, up_ref, down_ref)


VMEM = pl.BlockSpec(memory_space=pltpu.VMEM)
SMEM = pl.BlockSpec(memory_space=pltpu.SMEM)
ANY = pl.BlockSpec(memory_space=pl.ANY)
F32, BF16 = jnp.float32, jnp.bfloat16
FPLANE = ((PAIRS * FX * YB, FW * YW), BF16)
APLANE = ((len(KINDS), AW * YW, PAIRS * AX * YB), BF16)
FLINE = ((VIEWS, RANK * NZ, 2 * NZ), BF16)
ALINE = ((VIEWS, 2 * NZ, RANK * NZ), BF16)
MID = ((VIEWS, BX, QY, RANK * NZ), BF16)
SUMS = ((EX, EY, NZ), F32)
FLOPS = 2 * VIEWS * BX * QY * NZ * RANK * 3 * TAPS * 16


def call(kernel, outs, in_specs, scratch, flops, args):
    bytes_all = 1 if flops == 1 else sum(a.size * a.dtype.itemsize for a in args)
    return pl.pallas_call(
        kernel,
        out_shape=[jax.ShapeDtypeStruct(*out) for out in outs],
        in_specs=in_specs,
        out_specs=[VMEM] * len(outs),
        scratch_shapes=[
            pltpu.SemaphoreType.DMA((s,)) if isinstance(s, int) else pltpu.VMEM(*s) for s in scratch
        ],
        compiler_params=pltpu.CompilerParams(vmem_limit_bytes=VMEM_LIMIT),
        cost_estimate=pl.CostEstimate(flops=flops, bytes_accessed=bytes_all, transcendentals=0),
    )(*args)


def place(quarter, brick, bricks):
    return (quarter ^ (2 if brick >= bricks // 2 else 0)) * bricks + brick


def send(value, pairs):
    bricks = lax.axis_size("brick")
    perm = [(place(*a, bricks), place(*b, bricks)) for a, b in pairs]
    return lax.ppermute(value, ("view", "brick"), perm)


def to_xor(value, by):
    return lax.ppermute(value, "view", [(i, i ^ by) for i in range(VIEWS)])


def from_next_brick(value):
    bricks = lax.axis_size("brick")
    return send(value, [((q, (b + 1) % bricks), (q, b)) for b in range(bricks) for q in range(VIEWS)])


def exchange(axis, to_previous, to_next):
    bricks = lax.axis_size("brick")
    if axis == "brick":
        up = [((q, b), (q, b + 1)) for b in range(bricks - 1) for q in range(VIEWS)]
    else:
        up = [((q, b), (q + 1, b)) for b in range(bricks) for q in range(VIEWS - 1)]
    from_previous = send(to_next, up)
    from_next = send(to_previous, [(j, i) for i, j in up])
    return lax.optimization_barrier((from_previous, from_next))


def fold(value, from_previous, from_next, dim, skip):
    width, size = from_next.shape[dim], value.shape[dim]
    pads = [[(0, 0)] * 3 for _ in range(2)]
    pads[0][dim] = (skip, size - width - skip)
    pads[1][dim] = (size - width - skip, skip)
    return value + jnp.pad(from_previous, pads[0]) + jnp.pad(from_next, pads[1])


def gathered(own):
    across = to_xor(own, 2)
    return [own, to_xor(own, 1), across, to_xor(across, 1)]


def assemble_kernel(groups, quarter_ref, *refs):
    parts, out_ref, sems = refs[:VIEWS], refs[-2], refs[-1]
    copies = []
    for by, part in enumerate(parts):
        at = pl.multiple_of(QY * (quarter_ref[0] ^ by), QY)
        for start, row, rows in groups:
            copies.append(
                pltpu.make_async_copy(
                    part.at[pl.ds(start, rows)],
                    out_ref.at[pl.ds(row, rows), pl.ds(at, QY)],
                    sems.at[len(copies)],
                )
            )
    for copy in copies:
        copy.start()
    for copy in copies:
        copy.wait()


def assemble(quarter, parts, groups, result):
    begun = [] if result is None else [result]
    return pl.pallas_call(
        functools.partial(assemble_kernel, groups),
        out_shape=jax.ShapeDtypeStruct((BX, NY, NZ), F32),
        in_specs=[SMEM] + [ANY] * (VIEWS + len(begun)),
        out_specs=ANY,
        scratch_shapes=[pltpu.SemaphoreType.DMA((VIEWS * len(groups),))],
        input_output_aliases={1 + VIEWS: 0} if begun else {},
        compiler_params=pltpu.CompilerParams(vmem_limit_bytes=1024 * 1024),
        cost_estimate=pl.CostEstimate(flops=1, bytes_accessed=1, transcendentals=0),
    )(quarter[None], *parts, *begun)


def shards(start_estimate, observed, psf_taps, offsets, coverage):
    me = lax.axis_index("view")
    bricks = lax.axis_size("brick")
    quarter = me ^ (2 * (lax.axis_index("brick") // (bricks // 2)))

    small = jnp.concatenate([psf_taps.reshape(-1), offsets.astype(F32)])[None]
    smalls = jnp.concatenate([small] + [to_xor(small, by) for by in range(1, VIEWS)], axis=0)

    pieces = [lax.dynamic_slice_in_dim(observed[0], QY * (quarter ^ by), QY, 1) for by in range(VIEWS)]
    pieces, smalls = lax.optimization_barrier((pieces, smalls))
    here = [to_xor(piece, by) if by else piece for by, piece in enumerate(pieces)]
    across = lax.rem(lax.axis_index("brick") + 1, bricks // 2) == 0
    first = jnp.where(across, me ^ 2, me)
    beyond = [from_next_brick(tile) for tile in here[:HALF]]

    smalls = jnp.where(across, jnp.roll(smalls, HALF, axis=0), smalls)
    shifts = smalls[:, OFFSET].astype(jnp.int32)

    padded = jnp.pad(start_estimate, ((0, 0), (HY, HY), (0, 0)))
    estimate = lax.dynamic_slice_in_dim(padded, QY * quarter, EY, 1)
    edge = estimate.astype(BF16)
    covered = jnp.broadcast_to(coverage.reshape(1, VIEWS, 1).astype(BF16), (1, VIEWS, NZ))
    covered = jnp.pad(covered, ((0, 0), (0, EY - VIEWS), (0, 0)))
    before, after = exchange(
        "brick",
        jnp.concatenate([edge[:HX], covered], axis=0),
        jnp.concatenate([edge[BX - HX :], covered], axis=0),
    )
    covers = jnp.stack([rows[HX, :VIEWS, 0] for rows in (before, jnp.pad(covered, ((HX, 0), (0, 0), (0, 0))), after)])
    covers = covers.astype(F32)
    counts = jnp.maximum(jnp.sum(covers, axis=1), 1.0)
    row_counts = jnp.repeat(counts, jnp.array([HX, BX, HX]), total_repeat_length=EX)[:, None, None]
    estimate = jnp.concatenate([before[:HX].astype(F32), estimate, after[:HX].astype(F32)], axis=0)
    fplane, aplane, fline, aline = call(
        prepare_kernel, [FPLANE, APLANE, FLINE, ALINE], [SMEM] * 3, [], 1, (first[None], smalls, covers)
    )

    half = ((HALF, BX, QY, NZ), F32)
    blurred = call(
        blur_kernel,
        [half, half],
        [VMEM, VMEM, ANY],
        [MID, FLINE, 1],
        1,
        (estimate.astype(BF16), fplane, fline),
    )
    here[HALF:], beyond, blurred = lax.optimization_barrier((here[HALF:], beyond, blurred))
    beyond = beyond + [from_next_brick(tile) for tile in here[HALF:]]
    here = [jnp.where(across, here[by ^ 2], here[by]) for by in range(VIEWS)]
    tiles = list(zip(here, beyond))
    tile_scratch = lambda views: ((views, 2 * BX, QY, NZ), BF16)
    back_scratch = lambda views: ((views * RANK, BX, QY, NZ), BF16)
    terms = ()
    for part in range(2):
        first_view = part * HALF
        outs = [SUMS, ((2 * HX, EY, NZ), F32), ((2 * HX, EY, NZ), F32)] if part else [SUMS]
        own_tiles = [tile for pair in tiles[first_view : first_view + HALF] for tile in pair]
        terms = call(
            functools.partial(back_kernel, first_view, part == 1, 2 * HX),
            outs,
            [SMEM] + [ANY] * (1 + 2 * HALF) + [VMEM, ANY] + [VMEM] * part,
            [half, tile_scratch(HALF), APLANE, back_scratch(HALF), 3 * HALF + 1],
            FLOPS // 2,
            (shifts, blurred[part], *own_tiles, aline, aplane, *terms),
        )
    summed, to_previous, to_next = terms
    summed = fold(summed, *exchange("brick", to_previous, to_next), 0, 0)
    summed = fold(summed, *exchange("view", summed[:, : 2 * HY], summed[:, QY:]), 1, 0)
    estimate = estimate * summed / row_counts

    summed, to_previous, to_next = call(
        both_kernel,
        [SUMS, ((HX, EY, NZ), F32), ((HX, EY, NZ), F32)],
        [SMEM, VMEM, VMEM] + [ANY] * (3 + 2 * VIEWS),
        [MID, back_scratch(VIEWS), FLINE, ALINE, APLANE, tile_scratch(VIEWS), 3 + 2 * VIEWS],
        2 * FLOPS,
        (shifts, estimate.astype(BF16), fplane, fline, aline, aplane, *[tile for pair in tiles for tile in pair]),
    )
    own = summed[HX : HX + BX]
    inner = own[HX : BX - HX]
    from_quarters = exchange("view", inner[:, :HY], inner[:, EY - HY :])
    from_bricks = exchange("brick", to_previous, to_next)
    estimate = estimate[HX : HX + BX, HY : HY + QY] / counts[1]
    inner = estimate[HX : BX - HX] * fold(inner[:, HY : HY + QY], *from_quarters, 1, 0)
    outer = jnp.concatenate([own[:HX] + from_bricks[0], own[BX - HX :] + from_bricks[1]], axis=0)
    from_quarters = exchange("view", outer[:, :HY], outer[:, EY - HY :])
    outer = fold(outer[:, HY : HY + QY], *from_quarters, 1, 0)
    outer = jnp.concatenate([estimate[:HX], estimate[BX - HX :]], axis=0) * outer

    result = assemble(quarter, gathered(inner), ((0, HX, BX - 2 * HX),), None)
    return assemble(quarter, gathered(outer), ((0, 0, HX), (HX, BX - HX, HX)), result)


def solution(mesh):
    in_specs = (
        P("brick", None, None),
        P("view", "brick", None, None),
        P("view", None, None, None),
        P("view"),
        P(None, "brick"),
    )
    out_specs = P("brick", None, None)
    return jax.shard_map(shards, mesh=mesh, in_specs=in_specs, out_specs=out_specs, check_vma=False)
```

```python
import functools

import jax
import jax.numpy as jnp
from jax import lax
from jax.experimental import pallas as pl
from jax.experimental.pallas import tpu as pltpu
from jax.sharding import PartitionSpec as P

BX, NY, NZ = 32, 256, 128
VIEWS, RANK, TAPS = 4, 3, 15
QY = NY // VIEWS
HX = TAPS // 2
HY = 8
EX, EY = BX + 2 * HX, QY + 2 * HY
PAIRS = VIEWS * RANK
YB = 16
YW = 32
FX = 2
FW = FX + TAPS - 1
AX = 4
AW = AX + TAPS - 1
KINDS = (0, 1, 2, 6, 7)
ROWS = 8
HALF = VIEWS // 2
VMEM_LIMIT = 56 * 1024 * 1024
KX, KY, KZ, OFFSET = (d * RANK * TAPS for d in range(4))


def iota(shape, dim):
    return lax.broadcasted_iota(jnp.int32, shape, dim)


def split(value):
    high = value.astype(jnp.bfloat16)
    return high, (value - high.astype(jnp.float32)).astype(jnp.bfloat16)


def prepare_kernel(first_ref, small_ref, covers_ref, fplane_ref, aplane_ref, fline_ref, aline_ref):
    me = first_ref[0]

    def tap(base, pair, t):
        return small_ref[pair // RANK, base + (pair % RANK) * TAPS + t]

    def weight(side, pair):
        return covers_ref[side, me ^ (pair // RANK)]

    lane = iota((YB, 128), 1)
    t_y = (lane & (YW - 1)) - iota((YB, 128), 0) - 1
    group = lane >> 5
    for pair in range(PAIRS):
        y = jnp.zeros((YB, 128), jnp.float32)
        for t in range(TAPS):
            y = jnp.where(t_y == t, tap(KY, pair, t), y)
        for dx in range(FX):
            for column in range(FW * YW // 128):
                x = jnp.zeros((YB, 128), jnp.float32)
                for j in range(4):
                    t = 4 * column + j - dx
                    if 0 <= t < TAPS:
                        x = jnp.where(group == j, tap(KX, pair, t), x)
                row = (pair * FX + dx) * YB
                fplane_ref[row : row + YB, column * 128 : column * 128 + 128] = (x * y).astype(jnp.bfloat16)

    lane = iota((YW, 128), 1)
    t_y = iota((YW, 128), 0) - (lane & (YB - 1)) - 1
    group = lane >> 4
    for column in range(PAIRS // 2):
        pairs = (2 * column, 2 * column + 1)
        first = group < AX
        y = jnp.zeros((YW, 128), jnp.float32)
        for t in range(TAPS):
            y = jnp.where(t_y == t, jnp.where(first, tap(KY, pairs[0], t), tap(KY, pairs[1], t)), y)
        sided = [
            y * jnp.where(first, weight(side, pairs[0]), weight(side, pairs[1])) for side in range(3)
        ]
        for xw in range(AW):
            x = jnp.zeros((YW, 128), jnp.float32)
            for half in range(2):
                for dx in range(AX):
                    if 0 <= xw - dx < TAPS:
                        x = jnp.where(group == half * AX + dx, tap(KX, pairs[half], xw - dx), x)
            made = {}
            for kind, step in enumerate(KINDS):
                row = step * AX + xw
                side = 0 if row < HX else 1 if row < HX + BX else 2
                if side not in made:
                    made[side] = (x * sided[side]).astype(jnp.bfloat16)
                aplane_ref[kind, xw * YW : xw * YW + YW, column * 128 : column * 128 + 128] = made[side]

    t_z = iota((NZ, NZ), 0) - iota((NZ, NZ), 1) + TAPS // 2

    @pl.loop(0, VIEWS)
    def _(view):
        for term in range(RANK):
            forward = jnp.zeros((NZ, NZ), jnp.float32)
            adjoint = jnp.zeros((NZ, NZ), jnp.float32)
            for t in range(TAPS):
                k = small_ref[view, KZ + term * TAPS + t]
                forward = jnp.where(t_z == t, k, forward)
                adjoint = jnp.where(t_z == TAPS - 1 - t, k, adjoint)
            at = term * NZ
            high, low = split(forward)
            fline_ref[view, at : at + NZ, :NZ] = high
            fline_ref[view, at : at + NZ, NZ:] = low
            high, low = split(adjoint)
            aline_ref[view, :NZ, at : at + NZ] = high
            aline_ref[view, NZ:, at : at + NZ] = low


def forward_plane(ext_ref, plane_ref, mid_ref):
    @pl.loop(0, BX // (2 * FX), unroll=4)
    def _(step):
        x0 = step * (2 * FX)
        for y0 in range(0, QY, YB):
            parts = [
                ext_ref[pl.ds(x0 + part * FX, FW), y0 : y0 + YW, :].reshape(FW * YW, NZ)
                for part in range(2)
            ]
            made = jnp.dot(
                plane_ref[...],
                jnp.concatenate(parts, axis=1),
                preferred_element_type=jnp.float32,
            ).astype(jnp.bfloat16)
            for view in range(VIEWS):
                for term in range(RANK):
                    for part in range(2):
                        for dx in range(FX):
                            row = ((view * RANK + term) * FX + dx) * YB
                            mid_ref[
                                view, x0 + part * FX + dx, y0 : y0 + YB, term * NZ : (term + 1) * NZ
                            ] = made[row : row + YB, part * NZ : (part + 1) * NZ]


def forward_line(mid_ref, line_ref, view, x0):
    a = mid_ref[view, pl.ds(x0, ROWS)].reshape(ROWS * QY, RANK * NZ)
    made = jnp.dot(a, line_ref[view], preferred_element_type=jnp.float32)
    return made[:, :NZ] + made[:, NZ:]


def quotient_rows(tiles_ref, slot, start, blurred):
    merged = tiles_ref[slot, pl.ds(start, ROWS)].reshape(ROWS * QY, NZ)
    return (merged.astype(jnp.float32) / blurred).astype(jnp.bfloat16)


def adjoint_line(quotient, line_ref, back_ref, view, slot, x0):
    doubled = jnp.concatenate([quotient, quotient], axis=1)
    made = jnp.dot(doubled, line_ref[view], preferred_element_type=jnp.float32).astype(jnp.bfloat16)
    for term in range(RANK):
        back_ref[slot * RANK + term, pl.ds(x0, ROWS)] = made[:, term * NZ : (term + 1) * NZ].reshape(
            ROWS, QY, NZ
        )


def adjoint_plane(back_ref, plane_ref, out_ref, first_pair, pairs):
    columns = slice(first_pair * AX * YB, (first_pair + pairs) * AX * YB)

    for step in range(BX // AX):
        x0 = step * AX
        kind = min(step, 2) + max(step - 5, 0)
        for y0 in range(0, QY // 2, YB):
            starts = (y0, y0 + QY // 2)
            parts = [
                back_ref[:pairs, x0 : x0 + AX, at : at + YB, :].reshape(pairs * AX * YB, NZ)
                for at in starts
            ]
            made = jnp.dot(
                plane_ref[kind, :, columns],
                jnp.concatenate(parts, axis=1),
                preferred_element_type=jnp.float32,
            )
            for part, at in enumerate(starts):
                out_ref[x0 : x0 + AW, at : at + YW, :] += made[
                    :, part * NZ : (part + 1) * NZ
                ].reshape(AW, YW, NZ)


def edges(out_ref, up_ref, down_ref):
    rows = up_ref.shape[0]
    up_ref[...] = out_ref[:rows]
    down_ref[...] = out_ref[EX - rows :]


def tile_copy(tile_hbm, rows_ref, part, sem):
    return pltpu.make_async_copy(tile_hbm.at[pl.ds(0, BX)], rows_ref.at[pl.ds(part * BX, BX)], sem)


def blur_kernel(ext_ref, plane_ref, line_hbm, first_ref, last_ref, mid_ref, line_ref, sem):
    copy = pltpu.make_async_copy(line_hbm, line_ref, sem.at[0])
    copy.start()
    forward_plane(ext_ref, plane_ref, mid_ref)
    copy.wait()
    for view in range(VIEWS):
        out_ref = (first_ref, last_ref)[view // HALF]
        for x0 in range(0, BX, ROWS):
            blurred = forward_line(mid_ref, line_ref, view, x0)
            out_ref[view % HALF, pl.ds(x0, ROWS)] = blurred.reshape(ROWS, QY, NZ)


def back_kernel(first_view, begun, edge_rows, *refs):
    refs = list(refs)
    offsets_ref, blurred_hbm = refs[:2]
    tiles_hbm = refs[2 : 2 + 2 * HALF]
    line_ref, plane_hbm = refs[2 + 2 * HALF : 4 + 2 * HALF]
    rest = refs[4 + 2 * HALF :]
    before_ref = rest.pop(0) if begun else None
    out_refs = [rest.pop(0) for _ in range(3 if begun else 1)]
    blurred_ref, tiles_ref, plane_ref, back_ref, sems = rest
    out_ref = out_refs[0]
    copies = [
        [pltpu.make_async_copy(blurred_hbm.at[slot], blurred_ref.at[slot], sems.at[slot])]
        + [
            tile_copy(tiles_hbm[2 * slot + part], tiles_ref.at[slot], part, sems.at[HALF + 2 * slot + part])
            for part in range(2)
        ]
        for slot in range(HALF)
    ]
    plane_copy = pltpu.make_async_copy(plane_hbm, plane_ref, sems.at[3 * HALF])
    for copy in copies[0] + copies[1] + [plane_copy]:
        copy.start()
    out_ref[...] = before_ref[...] if begun else jnp.zeros_like(out_ref)
    for slot in range(HALF):
        view = first_view + slot
        offset = offsets_ref[view]
        for copy in copies[slot]:
            copy.wait()
        for x0 in range(0, BX, ROWS):
            blurred = blurred_ref[slot, pl.ds(x0, ROWS)].reshape(ROWS * QY, NZ)
            quotient = quotient_rows(tiles_ref, slot, offset + x0, blurred)
            adjoint_line(quotient, line_ref, back_ref, view, slot, x0)

    plane_copy.wait()
    adjoint_plane(back_ref, plane_ref, out_ref, first_view * RANK, HALF * RANK)
    if begun:
        edges(*out_refs)


def both_kernel(offsets_ref, ext_ref, fplane_ref, fline_hbm, aline_hbm, aplane_hbm, *refs):
    tiles_hbm = refs[: 2 * VIEWS]
    out_ref, up_ref, down_ref, mid_ref, back_ref, fline_ref, aline_ref, aplane_ref, tiles_ref, sems = refs[
        2 * VIEWS :
    ]
    line_copies = [
        pltpu.make_async_copy(fline_hbm, fline_ref, sems.at[0]),
        pltpu.make_async_copy(aline_hbm, aline_ref, sems.at[1]),
    ]
    plane_copy = pltpu.make_async_copy(aplane_hbm, aplane_ref, sems.at[2])
    tile_copies = [
        tile_copy(tiles_hbm[2 * view + part], tiles_ref.at[view], part, sems.at[3 + 2 * view + part])
        for view in range(VIEWS)
        for part in range(2)
    ]
    for copy in line_copies + tile_copies + [plane_copy]:
        copy.start()
    out_ref[...] = jnp.zeros_like(out_ref)
    forward_plane(ext_ref, fplane_ref, mid_ref)
    for copy in line_copies + tile_copies:
        copy.wait()
    for view in range(VIEWS):
        offset = offsets_ref[view]
        for x0 in range(0, BX, ROWS):
            blurred = forward_line(mid_ref, fline_ref, view, x0)
            quotient = quotient_rows(tiles_ref, view, offset + x0, blurred)
            adjoint_line(quotient, aline_ref, back_ref, view, view, x0)

    plane_copy.wait()
    adjoint_plane(back_ref, aplane_ref, out_ref, 0, PAIRS)
    edges(out_ref, up_ref, down_ref)


VMEM = pl.BlockSpec(memory_space=pltpu.VMEM)
SMEM = pl.BlockSpec(memory_space=pltpu.SMEM)
ANY = pl.BlockSpec(memory_space=pl.ANY)
F32, BF16 = jnp.float32, jnp.bfloat16
FPLANE = ((PAIRS * FX * YB, FW * YW), BF16)
APLANE = ((len(KINDS), AW * YW, PAIRS * AX * YB), BF16)
FLINE = ((VIEWS, RANK * NZ, 2 * NZ), BF16)
ALINE = ((VIEWS, 2 * NZ, RANK * NZ), BF16)
MID = ((VIEWS, BX, QY, RANK * NZ), BF16)
SUMS = ((EX, EY, NZ), F32)
FLOPS = 2 * VIEWS * BX * QY * NZ * RANK * 3 * TAPS * 16


def call(kernel, outs, in_specs, scratch, flops, args):
    bytes_all = 1 if flops == 1 else sum(a.size * a.dtype.itemsize for a in args)
    return pl.pallas_call(
        kernel,
        out_shape=[jax.ShapeDtypeStruct(*out) for out in outs],
        in_specs=in_specs,
        out_specs=[VMEM] * len(outs),
        scratch_shapes=[
            pltpu.SemaphoreType.DMA((s,)) if isinstance(s, int) else pltpu.VMEM(*s) for s in scratch
        ],
        compiler_params=pltpu.CompilerParams(vmem_limit_bytes=VMEM_LIMIT),
        cost_estimate=pl.CostEstimate(flops=flops, bytes_accessed=bytes_all, transcendentals=0),
    )(*args)


def place(quarter, brick, bricks):
    return (quarter ^ (2 if brick >= bricks // 2 else 0)) * bricks + brick


def send(value, pairs):
    bricks = lax.axis_size("brick")
    perm = [(place(*a, bricks), place(*b, bricks)) for a, b in pairs]
    return lax.ppermute(value, ("view", "brick"), perm)


def to_xor(value, by):
    return lax.ppermute(value, "view", [(i, i ^ by) for i in range(VIEWS)])


def from_next_brick(value):
    bricks = lax.axis_size("brick")
    return send(value, [((q, (b + 1) % bricks), (q, b)) for b in range(bricks) for q in range(VIEWS)])


def exchange(axis, to_previous, to_next):
    bricks = lax.axis_size("brick")
    if axis == "brick":
        up = [((q, b), (q, b + 1)) for b in range(bricks - 1) for q in range(VIEWS)]
    else:
        up = [((q, b), (q + 1, b)) for b in range(bricks) for q in range(VIEWS - 1)]
    from_previous = send(to_next, up)
    from_next = send(to_previous, [(j, i) for i, j in up])
    return lax.optimization_barrier((from_previous, from_next))


def fold(value, from_previous, from_next, dim, skip):
    width, size = from_next.shape[dim], value.shape[dim]
    pads = [[(0, 0)] * 3 for _ in range(2)]
    pads[0][dim] = (skip, size - width - skip)
    pads[1][dim] = (size - width - skip, skip)
    return value + jnp.pad(from_previous, pads[0]) + jnp.pad(from_next, pads[1])


def gathered(own):
    across = to_xor(own, 2)
    return [own, to_xor(own, 1), across, to_xor(across, 1)]


def assemble_kernel(groups, quarter_ref, *refs):
    parts, out_ref, sems = refs[:VIEWS], refs[-2], refs[-1]
    copies = []
    for by, part in enumerate(parts):
        at = pl.multiple_of(QY * (quarter_ref[0] ^ by), QY)
        for start, row, rows in groups:
            copies.append(
                pltpu.make_async_copy(
                    part.at[pl.ds(start, rows)],
                    out_ref.at[pl.ds(row, rows), pl.ds(at, QY)],
                    sems.at[len(copies)],
                )
            )
    for copy in copies:
        copy.start()
    for copy in copies:
        copy.wait()


def assemble(quarter, parts, groups, result):
    begun = [] if result is None else [result]
    return pl.pallas_call(
        functools.partial(assemble_kernel, groups),
        out_shape=jax.ShapeDtypeStruct((BX, NY, NZ), F32),
        in_specs=[SMEM] + [ANY] * (VIEWS + len(begun)),
        out_specs=ANY,
        scratch_shapes=[pltpu.SemaphoreType.DMA((VIEWS * len(groups),))],
        input_output_aliases={1 + VIEWS: 0} if begun else {},
        compiler_params=pltpu.CompilerParams(vmem_limit_bytes=1024 * 1024),
        cost_estimate=pl.CostEstimate(flops=1, bytes_accessed=1, transcendentals=0),
    )(quarter[None], *parts, *begun)


def shards(start_estimate, observed, psf_taps, offsets, coverage):
    me = lax.axis_index("view")
    bricks = lax.axis_size("brick")
    quarter = me ^ (2 * (lax.axis_index("brick") // (bricks // 2)))

    small = jnp.concatenate([psf_taps.reshape(-1), offsets.astype(F32)])[None]
    smalls = jnp.concatenate([small] + [to_xor(small, by) for by in range(1, VIEWS)], axis=0)

    pieces = [lax.dynamic_slice_in_dim(observed[0], QY * (quarter ^ by), QY, 1) for by in range(VIEWS)]
    pieces, smalls = lax.optimization_barrier((pieces, smalls))
    here = [to_xor(piece, by) if by else piece for by, piece in enumerate(pieces)]
    across = lax.rem(lax.axis_index("brick") + 1, bricks // 2) == 0
    first = jnp.where(across, me ^ 2, me)
    beyond = [from_next_brick(tile) for tile in here[:HALF]]

    smalls = jnp.where(across, jnp.roll(smalls, HALF, axis=0), smalls)
    shifts = smalls[:, OFFSET].astype(jnp.int32)

    padded = jnp.pad(start_estimate, ((0, 0), (HY, HY), (0, 0)))
    estimate = lax.dynamic_slice_in_dim(padded, QY * quarter, EY, 1)
    edge = estimate.astype(BF16)
    covered = jnp.broadcast_to(coverage.reshape(1, VIEWS, 1).astype(BF16), (1, VIEWS, NZ))
    covered = jnp.pad(covered, ((0, 0), (0, EY - VIEWS), (0, 0)))
    before, after = exchange(
        "brick",
        jnp.concatenate([edge[:HX], covered], axis=0),
        jnp.concatenate([edge[BX - HX :], covered], axis=0),
    )
    covers = jnp.stack([rows[HX, :VIEWS, 0] for rows in (before, jnp.pad(covered, ((HX, 0), (0, 0), (0, 0))), after)])
    covers = covers.astype(F32)
    counts = jnp.maximum(jnp.sum(covers, axis=1), 1.0)
    row_counts = jnp.repeat(counts, jnp.array([HX, BX, HX]), total_repeat_length=EX)[:, None, None]
    estimate = jnp.concatenate([before[:HX].astype(F32), estimate, after[:HX].astype(F32)], axis=0)
    fplane, aplane, fline, aline = call(
        prepare_kernel, [FPLANE, APLANE, FLINE, ALINE], [SMEM] * 3, [], 1, (first[None], smalls, covers)
    )

    here[HALF:], beyond, estimate = lax.optimization_barrier((here[HALF:], beyond, estimate))
    beyond = beyond + [from_next_brick(tile) for tile in here[HALF:]]
    half = ((HALF, BX, QY, NZ), F32)
    blurred = call(
        blur_kernel,
        [half, half],
        [VMEM, VMEM, ANY],
        [MID, FLINE, 1],
        1,
        (estimate.astype(BF16), fplane, fline),
    )
    here = [jnp.where(across, here[by ^ 2], here[by]) for by in range(VIEWS)]
    tiles = list(zip(here, beyond))
    tile_scratch = lambda views: ((views, 2 * BX, QY, NZ), BF16)
    back_scratch = lambda views: ((views * RANK, BX, QY, NZ), BF16)
    terms = ()
    for part in range(2):
        first_view = part * HALF
        outs = [SUMS, ((2 * HX, EY, NZ), F32), ((2 * HX, EY, NZ), F32)] if part else [SUMS]
        own_tiles = [tile for pair in tiles[first_view : first_view + HALF] for tile in pair]
        terms = call(
            functools.partial(back_kernel, first_view, part == 1, 2 * HX),
            outs,
            [SMEM] + [ANY] * (1 + 2 * HALF) + [VMEM, ANY] + [VMEM] * part,
            [half, tile_scratch(HALF), APLANE, back_scratch(HALF), 3 * HALF + 1],
            FLOPS // 2,
            (shifts, blurred[part], *own_tiles, aline, aplane, *terms),
        )
    summed, to_previous, to_next = terms
    summed = fold(summed, *exchange("brick", to_previous, to_next), 0, 0)
    summed = fold(summed, *exchange("view", summed[:, : 2 * HY], summed[:, QY:]), 1, 0)
    estimate = estimate * summed / row_counts

    summed, to_previous, to_next = call(
        both_kernel,
        [SUMS, ((HX, EY, NZ), F32), ((HX, EY, NZ), F32)],
        [SMEM, VMEM, VMEM] + [ANY] * (3 + 2 * VIEWS),
        [MID, back_scratch(VIEWS), FLINE, ALINE, APLANE, tile_scratch(VIEWS), 3 + 2 * VIEWS],
        2 * FLOPS,
        (shifts, estimate.astype(BF16), fplane, fline, aline, aplane, *[tile for pair in tiles for tile in pair]),
    )
    own = summed[HX : HX + BX]
    inner = own[HX : BX - HX]
    from_quarters = exchange("view", inner[:, :HY], inner[:, EY - HY :])
    from_bricks = exchange("brick", to_previous, to_next)
    estimate = estimate[HX : HX + BX, HY : HY + QY] / counts[1]
    inner = estimate[HX : BX - HX] * fold(inner[:, HY : HY + QY], *from_quarters, 1, 0)
    outer = jnp.concatenate([own[:HX] + from_bricks[0], own[BX - HX :] + from_bricks[1]], axis=0)
    from_quarters = exchange("view", outer[:, :HY], outer[:, EY - HY :])
    outer = fold(outer[:, HY : HY + QY], *from_quarters, 1, 0)
    outer = jnp.concatenate([estimate[:HX], estimate[BX - HX :]], axis=0) * outer

    result = assemble(quarter, gathered(inner), ((0, HX, BX - 2 * HX),), None)
    return assemble(quarter, gathered(outer), ((0, 0, HX), (HX, BX - HX, HX)), result)


def solution(mesh):
    in_specs = (
        P("brick", None, None),
        P("view", "brick", None, None),
        P("view", None, None, None),
        P("view"),
        P(None, "brick"),
    )
    out_specs = P("brick", None, None)
    return jax.shard_map(shards, mesh=mesh, in_specs=in_specs, out_specs=out_specs, check_vma=False)
```
